32 devices in a mesh: groups: 2 (over y), dap: 4 (over z), dp: 4 (over x, core).
Axes of the slice: x: 2, y: 2, z: 4, core: 2. Of those that a mesh axis runs over, the one named last changes fastest.
Arguments:
- pair: bfloat16 [8, 128, 16, 16], P(('groups', 'dp'), None, 'dap'), parts along dimension 0, may hold values from -6 to 6
- cotangent: bfloat16 [8, 128, 16, 16], P(('groups', 'dp'), None, 'dap'), parts along dimension 0, may hold values from -6 to 6
- proj_weight: bfloat16 [2, 512, 128], replicated, may hold values from -0.5 to 0.5
- proj_bias: float32 [2, 512], replicated, may hold values from -3 to 3
- gate_weight: bfloat16 [2, 128, 128], replicated, may hold values from -0.5 to 0.5
- out_weight: bfloat16 [2, 128, 128], replicated, may hold values from -0.5 to 0.5
- chan_bias: float32 [2, 2, 128], replicated, may hold values from -3 to 3
- norm_gain: float32 [2, 2, 128], replicated, may hold values from 0.25 to 1.75
- norm_shift: float32 [2, 2, 128], replicated, may hold values from -3 to 3
Outputs:
- grad_pair: bfloat16 [8, 128, 16, 16], P(('groups', 'dp'), None, 'dap'), parts along dimension 0
- grad_proj_weight: float32 [4, 512, 128], P('groups'), parts along dimension 0
- grad_proj_bias: float32 [4, 512], P('groups'), parts along dimension 0
- grad_gate_weight: float32 [4, 128, 128], P('groups'), parts along dimension 0
- grad_out_weight: float32 [4, 128, 128], P('groups'), parts along dimension 0
- grad_chan_bias: float32 [4, 2, 128], P('groups'), parts along dimension 0
- grad_norm_gain: float32 [4, 2, 128], P('groups'), parts along dimension 0
- grad_norm_shift: float32 [4, 2, 128], P('groups'), parts along dimension 0
The draws below stay inside these ranges and needn't reach their ends.
There are 2 independent parts, one for each index of `groups`. The reference program is written for one: setup_inputs(seed, part) draws one part's arguments, and reference() takes and returns one part's arrays. A program takes and returns all parts, laid end to end along the dimension named above; an argument that names none is the same for every part. Nothing has to cross between parts.
All inputs are finite; a program needn't handle non-finite values.
Results may differ from the reference program's by a relative error of at most 0.01.
Values may be sent and summed in bfloat16 or wider, within the bound.
A program may use at most 64 MiB of HBM per device.

```python
import jax
import jax.numpy as jnp
from jax import lax

C = 128
N = 16
B = 4


def block_levels(own_key, shape, pieces, low, top_value):
    def one(axis_at, parts):
        heights = jax.random.uniform(jax.random.fold_in(jax.random.fold_in(own_key, 6), axis_at), (parts,), jnp.float32, low / len(pieces), top_value / len(pieces))
        return jnp.repeat(jnp.exp(heights), shape[axis_at] // parts).reshape((-1,) + (1,) * (len(shape) - axis_at - 1))

    factor_of = one(*pieces[0])
    for cut in pieces[1:]:
        factor_of = factor_of * one(*cut)
    return factor_of


def bell_draw(stream_key, dims, scale, limit, pieces=(), kind=jnp.bfloat16):
    values = jax.random.normal(stream_key, dims, jnp.float32) * scale
    if len(pieces) > 0:
        values = block_levels(stream_key, dims, pieces, -0.22, 0.18) * values
    return jnp.clip(values, min=-limit, max=limit).astype(kind)


def setup_inputs(seed: int = 0, part: int = 0) -> dict:
    key_of = jax.random.split(jax.random.key(seed), 10)
    part_splits = jax.random.split(jax.random.fold_in(key_of[9], part), 10)
    return {
        "pair": bell_draw(part_splits[0], (B, C, N, N), 1.0, 6.0, ((0, 4), (2, 4))),
        "cotangent": bell_draw(part_splits[1], (B, C, N, N), 1.0, 6.0, ((0, 4), (2, 4))),
        "proj_weight": bell_draw(key_of[2], (2, 4 * C, C), C ** -0.5, 0.5),
        "proj_bias": bell_draw(key_of[3], (2, 4 * C), 0.5, 3.0, (), jnp.float32),
        "gate_weight": bell_draw(key_of[4], (2, C, C), C ** -0.5, 0.5),
        "out_weight": bell_draw(key_of[5], (2, C, C), C ** -0.5, 0.5),
        "chan_bias": bell_draw(key_of[6], (2, 2, C), 0.5, 3.0, (), jnp.float32),
        "norm_gain": jnp.clip(1.0 + 0.15 * jax.random.normal(key_of[7], (2, 2, C), jnp.float32), 0.25, 1.75),
        "norm_shift": bell_draw(key_of[8], (2, 2, C), 0.5, 3.0, (), jnp.float32),
    }


EPSILON = 1e-05

def normalize(values, scale_by, offset):
    average = lax.optimization_barrier(jnp.mean(values, axis=0, keepdims=True))
    centred = values - average
    variance = lax.optimization_barrier(jnp.mean(centred * centred, axis=0, keepdims=True))
    inverse = lax.rsqrt(variance + EPSILON)
    standard = centred * inverse
    return (standard * scale_by[:, None] + offset[:, None], standard, inverse)

def normalize_back(upstream, scale_by, standard, inverse):
    scaled = upstream * scale_by[:, None]
    adjusted = scaled - lax.optimization_barrier(jnp.mean(scaled, axis=0, keepdims=True)) - standard * lax.optimization_barrier(jnp.mean(scaled * standard, axis=0, keepdims=True))
    return (inverse * adjusted, lax.optimization_barrier(jnp.sum(upstream * standard, axis=1)), lax.optimization_barrier(jnp.sum(upstream, axis=1)))

def matmul_rows(left, right):
    return lax.dot_general(left, right, (((1,), (1,)), ((), ())), preferred_element_type=jnp.float32)

def matmul_cols(left, right):
    return lax.dot_general(left, right, (((0,), (0,)), ((), ())), preferred_element_type=jnp.float32)

def batched(form, left, right):
    return jnp.einsum(form, left.astype(jnp.float32), right.astype(jnp.float32), precision=lax.Precision.HIGHEST)

def forward_update(pair_rows, params, layer, width, incoming):
    proj_weight, proj_bias, gate_weight, out_weight, chan_bias, norm_gain, norm_shift = params
    channels = pair_rows.shape[0]
    source = pair_rows.astype(jnp.float32)
    normed, standard_in, inverse_in = normalize(source, norm_gain[layer, 0], norm_shift[layer, 0])
    inputs = normed.astype(jnp.bfloat16)
    pre_act = jnp.dot(proj_weight[layer], inputs, preferred_element_type=jnp.float32) + proj_bias[layer][:, None]
    left_value = pre_act[:channels]
    left_logit = pre_act[channels:2 * channels]
    right_value = pre_act[2 * channels:3 * channels]
    right_logit = pre_act[3 * channels:]
    left_full = (jax.nn.sigmoid(left_logit) * left_value).astype(jnp.bfloat16).reshape(channels, width, width)
    right_full = (jax.nn.sigmoid(right_logit) * right_value).astype(jnp.bfloat16).reshape(channels, width, width)
    gate = jax.nn.sigmoid(jnp.dot(gate_weight[layer], inputs, preferred_element_type=jnp.float32) + chan_bias[layer, 0][:, None])
    if incoming:
        triangle = batched('cki,ckj->cij', left_full, right_full)
    else:
        triangle = batched('cik,cjk->cij', left_full, right_full)
    triangle = triangle.astype(jnp.bfloat16).reshape(channels, width * width)
    normed_tri, standard_out, inverse_out = normalize(triangle.astype(jnp.float32), norm_gain[layer, 1], norm_shift[layer, 1])
    tri_inputs = normed_tri.astype(jnp.bfloat16)
    linear = jnp.dot(out_weight[layer], tri_inputs, preferred_element_type=jnp.float32) + chan_bias[layer, 1][:, None]
    next_pair = (source + gate * linear).astype(jnp.bfloat16)
    saved = (inputs, standard_in, inverse_in, left_value, left_logit, right_value, right_logit, left_full, right_full, gate, linear, tri_inputs, standard_out, inverse_out)
    return (next_pair, saved)

def backward_update(upstream, saved, params, layer, width, incoming):
    proj_weight, proj_bias, gate_weight, out_weight, chan_bias, norm_gain, norm_shift = params
    inputs, standard_in, inverse_in, left_value, left_logit, right_value, right_logit, left_full, right_full, gate, linear, tri_inputs, standard_out, inverse_out = saved
    channels = upstream.shape[0]
    grad_linear = (upstream * gate).astype(jnp.bfloat16)
    grad_logit = (upstream * linear * gate * (1.0 - gate)).astype(jnp.bfloat16)
    grad_out_w = matmul_rows(grad_linear, tri_inputs)
    grad_out_b = lax.optimization_barrier(jnp.sum(grad_linear.astype(jnp.float32), axis=1))
    grad_gate_w = matmul_rows(grad_logit, inputs)
    grad_gate_b = lax.optimization_barrier(jnp.sum(grad_logit.astype(jnp.float32), axis=1))
    grad_normed = matmul_cols(out_weight[layer], grad_linear)
    grad_tri, gain_out, shift_out = normalize_back(grad_normed, norm_gain[layer, 1], standard_out, inverse_out)
    grad_cube = grad_tri.astype(jnp.bfloat16).reshape(channels, width, width)
    if incoming:
        left_back = batched('ckj,cij->cki', right_full, grad_cube)
        right_back = batched('cki,cij->ckj', left_full, grad_cube)
    else:
        left_back = batched('cij,cjk->cik', grad_cube, right_full)
        right_back = batched('cij,cik->cjk', grad_cube, left_full)
    left_back = left_back.astype(jnp.bfloat16).reshape(channels, width * width).astype(jnp.float32)
    right_back = right_back.astype(jnp.bfloat16).reshape(channels, width * width).astype(jnp.float32)
    left_sig = jax.nn.sigmoid(left_logit)
    right_sig = jax.nn.sigmoid(right_logit)
    grad_pre = jnp.concatenate([left_back * left_sig, left_back * left_value * left_sig * (1.0 - left_sig), right_back * right_sig, right_back * right_value * right_sig * (1.0 - right_sig)], axis=0).astype(jnp.bfloat16)
    grad_proj_w = matmul_rows(grad_pre, inputs)
    grad_proj_b = lax.optimization_barrier(jnp.sum(grad_pre.astype(jnp.float32), axis=1))
    grad_inputs = matmul_cols(proj_weight[layer], grad_pre) + matmul_cols(gate_weight[layer], grad_logit)
    grad_source, gain_in, shift_in = normalize_back(grad_inputs, norm_gain[layer, 0], standard_in, inverse_in)
    grads = (grad_proj_w, grad_proj_b, grad_gate_w, grad_out_w, jnp.stack([grad_gate_b, grad_out_b]), jnp.stack([gain_in, gain_out]), jnp.stack([shift_in, shift_out]))
    return (upstream + grad_source, grads)

def reference(pair, cotangent, proj_weight, proj_bias, gate_weight, out_weight, chan_bias, norm_gain, norm_shift):
    params = (proj_weight, proj_bias, gate_weight, out_weight, chan_bias, norm_gain, norm_shift)

    def one_structure(operands):
        pair_one, cot_one = operands
        channels = pair_one.shape[0]
        width = pair_one.shape[1]
        start_pair = pair_one.reshape(channels, width * width)
        middle, saved_first = forward_update(start_pair, params, 0, width, False)
        unused, saved_second = forward_update(middle, params, 1, width, True)
        upstream = cot_one.reshape(channels, width * width).astype(jnp.float32)
        grad_middle, grads_second = backward_update(upstream, saved_second, params, 1, width, True)
        grad_start, grads_first = backward_update(grad_middle, saved_first, params, 0, width, False)
        stacked = tuple((jnp.stack([first_part, second_part]) for first_part, second_part in zip(grads_first, grads_second)))
        return (grad_start.astype(jnp.bfloat16).reshape(pair_one.shape),) + stacked
    results = lax.map(one_structure, (pair, cotangent))
    factor = 1.0 / pair.shape[-1]
    return (results[0], lax.optimization_barrier(jnp.sum(results[1], axis=0)) * factor, lax.optimization_barrier(jnp.sum(results[2], axis=0)) * factor, lax.optimization_barrier(jnp.sum(results[3], axis=0)) * factor, lax.optimization_barrier(jnp.sum(results[4], axis=0)) * factor, lax.optimization_barrier(jnp.sum(results[5], axis=0)) * factor, lax.optimization_barrier(jnp.sum(results[6], axis=0)) * factor, lax.optimization_barrier(jnp.sum(results[7], axis=0)) * factor)
```

```python
import functools

import jax
import jax.numpy as jnp
from jax import lax
from jax.experimental import pallas as pl
from jax.experimental.pallas import tpu as pltpu
from jax.sharding import PartitionSpec as P

EPSILON = 1e-05


def normalize(values, scale_by, offset):
    average = jnp.mean(values, axis=0, keepdims=True)
    centred = values - average
    variance = jnp.mean(centred * centred, axis=0, keepdims=True)
    inverse = lax.rsqrt(variance + EPSILON)
    standard = centred * inverse
    return (standard * scale_by[:, None] + offset[:, None], standard, inverse)


def normalize_back(upstream, scale_by, standard, inverse):
    scaled = upstream * scale_by[:, None]
    adjusted = (
        scaled
        - jnp.mean(scaled, axis=0, keepdims=True)
        - standard * jnp.mean(scaled * standard, axis=0, keepdims=True)
    )
    return (inverse * adjusted, jnp.sum(upstream * standard, axis=1), jnp.sum(upstream, axis=1))


def matmul_rows(left, right):
    return lax.dot_general(
        left, right, (((1,), (1,)), ((), ())), preferred_element_type=jnp.float32
    )


def matmul_cols(left, right):
    return lax.dot_general(
        left, right, (((0,), (0,)), ((), ())), preferred_element_type=jnp.float32
    )


def contract(left, right, left_dim, right_dim):
    return lax.dot_general(
        left, right, (((left_dim,), (right_dim,)), ((0,), (0,))), preferred_element_type=jnp.float32
    )


def forward_update(pair_rows, params, layer, dims, incoming):
    proj_weight, proj_bias, gate_weight, out_weight, chan_bias, norm_gain, norm_shift = params
    channels, rows, width = dims
    source = pair_rows.astype(jnp.float32)
    normed, standard_in, inverse_in = normalize(source, norm_gain[layer, 0], norm_shift[layer, 0])
    inputs = normed.astype(jnp.bfloat16)
    weight_now = proj_weight[layer]
    bias_now = proj_bias[layer]

    def gated(first_row):
        pre_act = jnp.dot(
            weight_now[first_row : first_row + 2 * channels],
            inputs,
            preferred_element_type=jnp.float32,
        )
        pre_act = pre_act + bias_now[first_row : first_row + 2 * channels][:, None]
        value = pre_act[:channels]
        logit = pre_act[channels:]
        product = (
            (jax.nn.sigmoid(logit) * value).astype(jnp.bfloat16).reshape(channels, rows, width)
        )
        return (product, value, logit)

    left_rows, left_value, left_logit = gated(0)
    left_cols = lax.all_to_all(left_rows, "dap", split_axis=0, concat_axis=1, tiled=True)
    right_rows, right_value, right_logit = gated(2 * channels)
    right_cols = lax.all_to_all(right_rows, "dap", split_axis=0, concat_axis=1, tiled=True)
    gate = jax.nn.sigmoid(
        jnp.dot(gate_weight[layer], inputs, preferred_element_type=jnp.float32)
        + chan_bias[layer, 0][:, None]
    )
    if incoming:
        triangle = contract(left_cols, right_cols, 1, 1)
    else:
        triangle = contract(left_cols, right_cols, 2, 2)
    triangle_rows = lax.all_to_all(
        triangle.astype(jnp.bfloat16), "dap", split_axis=1, concat_axis=0, tiled=True
    )
    triangle_rows = triangle_rows.reshape(channels, rows * width)
    normed_tri, standard_out, inverse_out = normalize(
        triangle_rows.astype(jnp.float32), norm_gain[layer, 1], norm_shift[layer, 1]
    )
    tri_inputs = normed_tri.astype(jnp.bfloat16)
    linear = (
        jnp.dot(out_weight[layer], tri_inputs, preferred_element_type=jnp.float32)
        + chan_bias[layer, 1][:, None]
    )
    next_pair = (source + gate * linear).astype(jnp.bfloat16)
    saved = (
        inputs,
        standard_in,
        inverse_in,
        left_value,
        left_logit,
        right_value,
        right_logit,
        left_cols,
        right_cols,
        gate,
        linear,
        tri_inputs,
        standard_out,
        inverse_out,
    )
    return (next_pair, saved)


def backward_update(upstream, saved, params, layer, dims, incoming):
    proj_weight, proj_bias, gate_weight, out_weight, chan_bias, norm_gain, norm_shift = params
    channels, rows, width = dims
    (
        inputs,
        standard_in,
        inverse_in,
        left_value,
        left_logit,
        right_value,
        right_logit,
        left_cols,
        right_cols,
        gate,
        linear,
        tri_inputs,
        standard_out,
        inverse_out,
    ) = saved
    grad_linear = (upstream * gate).astype(jnp.bfloat16)
    grad_logit = (upstream * linear * gate * (1.0 - gate)).astype(jnp.bfloat16)
    grad_out_w = matmul_rows(grad_linear, tri_inputs)
    grad_out_b = jnp.sum(grad_linear.astype(jnp.float32), axis=1)
    grad_gate_w = matmul_rows(grad_logit, inputs)
    grad_gate_b = jnp.sum(grad_logit.astype(jnp.float32), axis=1)
    grad_normed = matmul_cols(out_weight[layer], grad_linear)
    grad_tri, gain_out, shift_out = normalize_back(
        grad_normed, norm_gain[layer, 1], standard_out, inverse_out
    )
    grad_cols = lax.all_to_all(
        grad_tri.astype(jnp.bfloat16).reshape(channels, rows, width),
        "dap",
        split_axis=0,
        concat_axis=1,
        tiled=True,
    )

    def left_term():
        if incoming:
            return contract(right_cols, grad_cols, 2, 2).astype(jnp.bfloat16)
        return contract(grad_cols, right_cols, 2, 1).astype(jnp.bfloat16)

    def right_term():
        if incoming:
            return contract(left_cols, grad_cols, 2, 1).astype(jnp.bfloat16)
        return contract(grad_cols, left_cols, 1, 1).astype(jnp.bfloat16)

    left_back = lax.all_to_all(left_term(), "dap", split_axis=1, concat_axis=0, tiled=True)
    right_back = lax.all_to_all(right_term(), "dap", split_axis=1, concat_axis=0, tiled=True)
    left_back = left_back.reshape(channels, rows * width).astype(jnp.float32)
    right_back = right_back.reshape(channels, rows * width).astype(jnp.float32)
    left_sig = jax.nn.sigmoid(left_logit)
    right_sig = jax.nn.sigmoid(right_logit)
    grad_pre = jnp.concatenate(
        [
            left_back * left_sig,
            left_back * left_value * left_sig * (1.0 - left_sig),
            right_back * right_sig,
            right_back * right_value * right_sig * (1.0 - right_sig),
        ],
        axis=0,
    ).astype(jnp.bfloat16)
    grad_proj_w = matmul_rows(grad_pre, inputs)
    grad_proj_b = jnp.sum(grad_pre.astype(jnp.float32), axis=1)
    grad_inputs = matmul_cols(proj_weight[layer], grad_pre) + matmul_cols(
        gate_weight[layer], grad_logit
    )
    grad_source, gain_in, shift_in = normalize_back(
        grad_inputs, norm_gain[layer, 0], standard_in, inverse_in
    )
    grads = (
        grad_proj_w,
        grad_proj_b,
        grad_gate_w,
        grad_out_w,
        jnp.stack([grad_gate_b, grad_out_b]),
        jnp.stack([gain_in, gain_out]),
        jnp.stack([shift_in, shift_out]),
    )
    return (upstream + grad_source, grads)


def large_body(
    pair,
    cotangent,
    proj_weight,
    proj_bias,
    gate_weight,
    out_weight,
    chan_bias,
    norm_gain,
    norm_shift,
):
    params = (proj_weight, proj_bias, gate_weight, out_weight, chan_bias, norm_gain, norm_shift)
    channels = pair.shape[1]
    rows = pair.shape[2]
    width = pair.shape[3]
    dims = (channels, rows, width)
    start_pair = pair[0].reshape(channels, rows * width)
    middle, saved_first = forward_update(start_pair, params, 0, dims, False)
    unused, saved_second = forward_update(middle, params, 1, dims, True)
    upstream = cotangent[0].reshape(channels, rows * width).astype(jnp.float32)
    grad_middle, grads_second = backward_update(upstream, saved_second, params, 1, dims, True)
    repeat_pair, saved_first = forward_update(start_pair, params, 0, dims, False)
    grad_start, grads_first = backward_update(grad_middle, saved_first, params, 0, dims, False)
    joined = tuple(
        (
            jnp.stack([first_part, second_part])
            for first_part, second_part in zip(grads_first, grads_second)
        )
    )
    stacked = lax.psum(
        (joined[0], joined[1], joined[2], joined[3], joined[4], joined[5], joined[6]), ("dap", "dp")
    )
    factor = 1.0 / width
    return (
        grad_start.astype(jnp.bfloat16).reshape(1, channels, rows, width),
        stacked[0] * factor,
        stacked[1] * factor,
        stacked[2] * factor,
        stacked[3] * factor,
        stacked[4] * factor,
        stacked[5] * factor,
        stacked[6] * factor,
    )


def norm_lanes(values, scale_by, offset):
    average = jnp.mean(values, axis=1, keepdims=True)
    centred = values - average
    variance = jnp.mean(centred * centred, axis=1, keepdims=True)
    inverse = lax.rsqrt(variance + EPSILON)
    standard = centred * inverse
    return (standard * scale_by + offset, standard, inverse)


def norm_lanes_back(upstream, scale_by, standard, inverse):
    scaled = upstream * scale_by
    adjusted = (
        scaled
        - jnp.mean(scaled, axis=1, keepdims=True)
        - standard * jnp.mean(scaled * standard, axis=1, keepdims=True)
    )
    return inverse * adjusted


def column_sum(values):
    return jnp.sum(values, axis=0, keepdims=True)


def rounded(values):
    return values.astype(jnp.bfloat16).astype(jnp.float32)


def products(width, a_ref, a_turned, b_ref, b_turned, o_ref):
    blocks = [
        b_ref[pl.ds(m, width, stride=width), :] if b_turned else b_ref[pl.ds(m * width, width), :]
        for m in range(width)
    ]

    def step(p, carry):
        total = None
        for m in range(width):
            row = a_ref[pl.ds(m * width + p if a_turned else p * width + m, 1), :]
            term = row * blocks[m]
            total = term if total is None else total + term
        o_ref[pl.ds(pl.multiple_of(p * width, width), width), :] = total
        return carry

    lax.fori_loop(0, width, step, 0)


def fused_kernel(
    peers,
    width,
    pair_ref,
    cot_ref,
    proj_ref,
    gate_ref,
    outw_ref,
    bias_ref,
    chan_ref,
    gain_ref,
    shift_ref,
    dpair_ref,
    big_ref,
    small_ref,
    pair_all,
    cot_all,
    left_s,
    right_s,
    tri_s,
    grad_s,
    dleft_s,
    dright_s,
    rows_s,
    send_half,
    recv_half,
    send_sum,
    recv_sum,
    small_all,
    gather_send,
    gather_recv,
    half_send,
    half_recv,
    sum_send,
    sum_recv,
    share_send,
    share_recv,
    small_send,
    small_recv,
):
    dap, dp = peers
    mesh_ids = pl.DeviceIdType.MESH
    channels = pair_ref.shape[1]
    held = pair_ref.shape[0]
    me = lax.axis_index("dap")
    at = lax.axis_index("dp")
    core = lax.rem(at, 2)
    core_peer = at + 1 - 2 * core
    far_peer = lax.rem(at + 2, dp)

    barrier = pltpu.get_barrier_semaphore()
    for k in range(1, dap):
        pl.semaphore_signal(
            barrier, inc=1, device_id={"dap": lax.rem(me + k, dap)}, device_id_type=mesh_ids
        )
    for k in range(1, dp):
        pl.semaphore_signal(
            barrier, inc=1, device_id={"dp": lax.rem(at + k, dp)}, device_id_type=mesh_ids
        )
    pl.semaphore_wait(barrier, dap + dp - 2)

    own = pl.ds(pl.multiple_of(me * held, held), held)
    gathers = []
    for slot, (source, whole) in enumerate(((pair_ref, pair_all), (cot_ref, cot_all))):
        copies = []
        for k in range(1, dap):
            copy = pltpu.make_async_remote_copy(
                src_ref=source,
                dst_ref=whole.at[own],
                send_sem=gather_send.at[slot, k - 1],
                recv_sem=gather_recv.at[slot, k - 1],
                device_id={"dap": lax.rem(me + k, dap)},
                device_id_type=mesh_ids,
            )
            copy.start()
            copies.append(copy)
        gathers.append(copies)
        whole[own, :] = source[...]

    factor = 1.0 / width

    def forward(source, layer):
        normed, standard_in, inverse_in = norm_lanes(
            source, gain_ref[layer, 0:1, :], shift_ref[layer, 0:1, :]
        )
        inputs = normed.astype(jnp.bfloat16)
        pre_act = matmul_rows(inputs, proj_ref[layer]) + bias_ref[layer : layer + 1, :]
        left_value = pre_act[:, :channels]
        left_sig = jax.nn.sigmoid(pre_act[:, channels : 2 * channels])
        right_value = pre_act[:, 2 * channels : 3 * channels]
        right_sig = jax.nn.sigmoid(pre_act[:, 3 * channels :])
        left_s[layer] = rounded(left_sig * left_value)
        right_s[layer] = rounded(right_sig * right_value)
        gate = jax.nn.sigmoid(matmul_rows(inputs, gate_ref[layer]) + chan_ref[layer, 0:1, :])
        left, right = left_s.at[layer], right_s.at[layer]
        if layer == 0:
            products(width, left, False, right, True, tri_s)
        else:
            products(width, left, True, right, False, tri_s)
        normed_tri, standard_out, inverse_out = norm_lanes(
            rounded(tri_s[...]), gain_ref[layer, 1:2, :], shift_ref[layer, 1:2, :]
        )
        tri_inputs = normed_tri.astype(jnp.bfloat16)
        linear = matmul_rows(tri_inputs, outw_ref[layer]) + chan_ref[layer, 1:2, :]
        saved = (
            inputs,
            standard_in,
            inverse_in,
            left_value,
            left_sig,
            right_value,
            right_sig,
            gate,
            linear,
            tri_inputs,
            standard_out,
            inverse_out,
        )
        return saved

    def put_small(layer, row, values):
        rows_s[layer, row : row + 1, :] = values * factor

    def backward_near(upstream, saved, layer):
        inputs, _, _, _, _, _, _, gate, linear, tri_inputs, standard_out, inverse_out = saved
        grad_linear = (upstream * gate).astype(jnp.bfloat16)
        grad_logit = (upstream * linear * gate * (1.0 - gate)).astype(jnp.bfloat16)
        grad_normed = jnp.dot(grad_linear, outw_ref[layer], preferred_element_type=jnp.float32)
        grad_s[...] = rounded(
            norm_lanes_back(grad_normed, gain_ref[layer, 1:2, :], standard_out, inverse_out)
        )
        big_ref[layer, 4 * channels : 5 * channels, :] = matmul_cols(grad_logit, inputs) * factor
        big_ref[layer, 5 * channels :, :] = matmul_cols(grad_linear, tri_inputs) * factor
        put_small(layer, 4, column_sum(grad_logit.astype(jnp.float32)))
        put_small(layer, 5, column_sum(grad_linear.astype(jnp.float32)))
        put_small(layer, 7, column_sum(grad_normed * standard_out))
        put_small(layer, 9, column_sum(grad_normed))
        return grad_logit

    def backward_far(upstream, saved, grad_logit, layer):
        inputs, standard_in, inverse_in, left_value, left_sig, right_value, right_sig = saved[:7]
        left, right = left_s.at[layer], right_s.at[layer]
        if layer == 0:
            products(width, grad_s, False, right, False, dleft_s)
            products(width, grad_s, True, left, False, dright_s)
        else:
            products(width, right, False, grad_s, True, dleft_s)
            products(width, left, False, grad_s, False, dright_s)
        left_back = rounded(dleft_s[...])
        right_back = rounded(dright_s[...])
        blocks = (
            left_back * left_sig,
            left_back * left_value * left_sig * (1.0 - left_sig),
            right_back * right_sig,
            right_back * right_value * right_sig * (1.0 - right_sig),
        )
        grad_inputs = jnp.dot(grad_logit, gate_ref[layer], preferred_element_type=jnp.float32)
        for index, block in enumerate(blocks):
            part = block.astype(jnp.bfloat16)
            lines = slice(index * channels, (index + 1) * channels)
            big_ref[layer, lines, :] = matmul_cols(part, inputs) * factor
            put_small(layer, index, column_sum(part.astype(jnp.float32)))
            grad_inputs = grad_inputs + jnp.dot(
                part, proj_ref[layer, lines, :], preferred_element_type=jnp.float32
            )
        put_small(layer, 6, column_sum(grad_inputs * standard_in))
        put_small(layer, 8, column_sum(grad_inputs))
        return upstream + norm_lanes_back(
            grad_inputs, gain_ref[layer, 0:1, :], standard_in, inverse_in
        )

    pieces = (
        (1, 0, 6 * channels),
        (0, 4 * channels, 2 * channels),
        (0, 0, 4 * channels),
    )
    flights = {}

    def spans(index):
        layer, first, count = pieces[index]
        half = count // 2
        mine = pl.ds(pl.multiple_of(first + core * half, half), half)
        other = pl.ds(pl.multiple_of(first + (1 - core) * half, half), half)
        slot = pl.ds(sum(piece[2] // 2 for piece in pieces[:index]), half)
        return (big_ref.at[layer], mine, other, slot)

    def exchange_half(index):
        whole, mine, other, slot = spans(index)
        send_half[slot, :] = whole[other, :].astype(jnp.bfloat16)
        copy = pltpu.make_async_remote_copy(
            src_ref=send_half.at[slot],
            dst_ref=recv_half.at[slot],
            send_sem=half_send.at[index],
            recv_sem=half_recv.at[index],
            device_id={"dp": core_peer},
            device_id_type=mesh_ids,
        )
        copy.start()
        flights[index] = [copy]

    def exchange_sum(index):
        whole, mine, other, slot = spans(index)
        flights[index][0].wait_recv()
        added = whole[mine, :] + recv_half[slot, :].astype(jnp.float32)
        send_sum[slot, :] = added.astype(jnp.bfloat16)
        copy = pltpu.make_async_remote_copy(
            src_ref=send_sum.at[slot],
            dst_ref=recv_sum.at[slot],
            send_sem=sum_send.at[index],
            recv_sem=sum_recv.at[index],
            device_id={"dp": far_peer},
            device_id_type=mesh_ids,
        )
        copy.start()
        flights[index].append(copy)

    def share(index):
        whole, mine, other, slot = spans(index)
        flights[index][1].wait_recv()
        whole[mine, :] = send_sum[slot, :].astype(jnp.float32) + recv_sum[slot, :].astype(
            jnp.float32
        )
        copy = pltpu.make_async_remote_copy(
            src_ref=whole.at[mine],
            dst_ref=whole.at[mine],
            send_sem=share_send.at[index],
            recv_sem=share_recv.at[index],
            device_id={"dp": core_peer},
            device_id_type=mesh_ids,
        )
        copy.start()
        flights[index].append(copy)

    for copy in gathers[0]:
        copy.wait_recv()
    start_pair = pair_all[...].astype(jnp.float32)
    saved_first = forward(start_pair, 0)
    middle = rounded(start_pair + saved_first[7] * saved_first[8])
    saved_second = forward(middle, 1)
    for copy in gathers[1]:
        copy.wait_recv()
    upstream = cot_all[...].astype(jnp.float32)
    grad_logit = backward_near(upstream, saved_second, 1)
    grad_middle = backward_far(upstream, saved_second, grad_logit, 1)
    exchange_half(0)
    grad_logit = backward_near(grad_middle, saved_first, 0)
    exchange_half(1)
    exchange_sum(0)
    grad_start = backward_far(grad_middle, saved_first, grad_logit, 0)
    exchange_half(2)
    small_all[at] = rows_s[...]
    small_copies = []
    for k in range(1, dp):
        copy = pltpu.make_async_remote_copy(
            src_ref=rows_s,
            dst_ref=small_all.at[at],
            send_sem=small_send.at[k - 1],
            recv_sem=small_recv.at[k - 1],
            device_id={"dp": lax.rem(at + k, dp)},
            device_id_type=mesh_ids,
        )
        copy.start()
        small_copies.append(copy)
    exchange_sum(1)
    exchange_sum(2)
    dleft_s[...] = grad_start
    dpair_ref[...] = dleft_s[own, :].astype(jnp.bfloat16)
    share(0)
    share(1)
    for copy in small_copies:
        copy.wait_recv()
    total = small_all[0]
    for index in range(1, dp):
        total = total + small_all[index]
    small_ref[...] = total
    share(2)
    for index in range(3):
        flights[index][2].wait_recv()
    for index in range(3):
        for copy in flights[index]:
            copy.wait_send()
    for copy in gathers[0] + gathers[1] + small_copies:
        copy.wait_send()


def fused_body(
    peers,
    pair,
    cotangent,
    proj_weight,
    proj_bias,
    gate_weight,
    out_weight,
    chan_bias,
    norm_gain,
    norm_shift,
):
    dap, dp = peers
    _, channels, rows, width = pair.shape
    held = rows * width
    entries = width * width
    float_rows = pltpu.VMEM((entries, channels), jnp.float32)
    layer_rows = pltpu.VMEM((2, entries, channels), jnp.float32)
    half_rows = pltpu.VMEM((6 * channels, channels), jnp.bfloat16)
    vmem = pl.BlockSpec(memory_space=pltpu.VMEM)
    grad_rows, big, small = pl.pallas_call(
        functools.partial(fused_kernel, peers, width),
        out_shape=(
            jax.ShapeDtypeStruct((held, channels), jnp.bfloat16),
            jax.ShapeDtypeStruct((2, 6 * channels, channels), jnp.float32),
            jax.ShapeDtypeStruct((2, 10, channels), jnp.float32),
        ),
        in_specs=[vmem] * 9,
        out_specs=(vmem, vmem, vmem),
        scratch_shapes=[
            pltpu.VMEM((entries, channels), jnp.bfloat16),
            pltpu.VMEM((entries, channels), jnp.bfloat16),
            layer_rows,
            layer_rows,
            float_rows,
            float_rows,
            float_rows,
            float_rows,
            pltpu.VMEM((2, 10, channels), jnp.float32),
            half_rows,
            half_rows,
            half_rows,
            half_rows,
            pltpu.VMEM((dp, 2, 10, channels), jnp.float32),
            pltpu.SemaphoreType.DMA((2, dap - 1)),
            pltpu.SemaphoreType.DMA((2, dap - 1)),
            pltpu.SemaphoreType.DMA((3,)),
            pltpu.SemaphoreType.DMA((3,)),
            pltpu.SemaphoreType.DMA((3,)),
            pltpu.SemaphoreType.DMA((3,)),
            pltpu.SemaphoreType.DMA((3,)),
            pltpu.SemaphoreType.DMA((3,)),
            pltpu.SemaphoreType.DMA((dp - 1,)),
            pltpu.SemaphoreType.DMA((dp - 1,)),
        ],
        compiler_params=pltpu.CompilerParams(
            collective_id=0, has_side_effects=True, vmem_limit_bytes=40 * 1024 * 1024
        ),
        name="triangle_updates",
    )(
        pair[0].reshape(channels, held).T,
        cotangent[0].reshape(channels, held).T,
        proj_weight,
        gate_weight,
        out_weight,
        proj_bias,
        chan_bias,
        norm_gain,
        norm_shift,
    )
    return (
        grad_rows.T.reshape(1, channels, rows, width),
        big[:, : 4 * channels],
        small[:, :4].reshape(2, 4 * channels),
        big[:, 4 * channels : 5 * channels],
        big[:, 5 * channels :],
        small[:, 4:6],
        small[:, 6:8],
        small[:, 8:10],
    )


def any_body(peers, pair, *others):
    _, channels, rows, width = pair.shape
    small = channels == 128 and width == 16 and rows % 4 == 0
    if small and peers[1] == 4 and peers[0] > 1:
        return fused_body(peers, pair, *others)
    return large_body(pair, *others)


def solution(mesh):
    in_specs = (
        P(("groups", "dp"), None, "dap", None),
        P(("groups", "dp"), None, "dap", None),
        P(),
        P(),
        P(),
        P(),
        P(),
        P(),
        P(),
    )
    out_specs = (
        P(("groups", "dp"), None, "dap", None),
        P("groups", None, None),
        P("groups", None),
        P("groups", None, None),
        P("groups", None, None),
        P("groups", None, None),
        P("groups", None, None),
        P("groups", None, None),
    )
    peers = (mesh.shape["dap"], mesh.shape["dp"])
    body = functools.partial(any_body, peers)
    return jax.shard_map(body, mesh=mesh, in_specs=in_specs, out_specs=out_specs, check_vma=False)
```

```python
import functools

import jax
import jax.numpy as jnp
from jax import lax
from jax.experimental import pallas as pl
from jax.experimental.pallas import tpu as pltpu
from jax.sharding import PartitionSpec as P

EPSILON = 1e-05


def normalize(values, scale_by, offset):
    average = jnp.mean(values, axis=0, keepdims=True)
    centred = values - average
    variance = jnp.mean(centred * centred, axis=0, keepdims=True)
    inverse = lax.rsqrt(variance + EPSILON)
    standard = centred * inverse
    return (standard * scale_by[:, None] + offset[:, None], standard, inverse)


def normalize_back(upstream, scale_by, standard, inverse):
    scaled = upstream * scale_by[:, None]
    adjusted = (
        scaled
        - jnp.mean(scaled, axis=0, keepdims=True)
        - standard * jnp.mean(scaled * standard, axis=0, keepdims=True)
    )
    return (inverse * adjusted, jnp.sum(upstream * standard, axis=1), jnp.sum(upstream, axis=1))


def matmul_rows(left, right):
    return lax.dot_general(
        left, right, (((1,), (1,)), ((), ())), preferred_element_type=jnp.float32
    )


def matmul_cols(left, right):
    return lax.dot_general(
        left, right, (((0,), (0,)), ((), ())), preferred_element_type=jnp.float32
    )


def contract(left, right, left_dim, right_dim):
    return lax.dot_general(
        left, right, (((left_dim,), (right_dim,)), ((0,), (0,))), preferred_element_type=jnp.float32
    )


def forward_update(pair_rows, params, layer, dims, incoming):
    proj_weight, proj_bias, gate_weight, out_weight, chan_bias, norm_gain, norm_shift = params
    channels, rows, width = dims
    source = pair_rows.astype(jnp.float32)
    normed, standard_in, inverse_in = normalize(source, norm_gain[layer, 0], norm_shift[layer, 0])
    inputs = normed.astype(jnp.bfloat16)
    weight_now = proj_weight[layer]
    bias_now = proj_bias[layer]

    def gated(first_row):
        pre_act = jnp.dot(
            weight_now[first_row : first_row + 2 * channels],
            inputs,
            preferred_element_type=jnp.float32,
        )
        pre_act = pre_act + bias_now[first_row : first_row + 2 * channels][:, None]
        value = pre_act[:channels]
        logit = pre_act[channels:]
        product = (
            (jax.nn.sigmoid(logit) * value).astype(jnp.bfloat16).reshape(channels, rows, width)
        )
        return (product, value, logit)

    left_rows, left_value, left_logit = gated(0)
    left_cols = lax.all_to_all(left_rows, "dap", split_axis=0, concat_axis=1, tiled=True)
    right_rows, right_value, right_logit = gated(2 * channels)
    right_cols = lax.all_to_all(right_rows, "dap", split_axis=0, concat_axis=1, tiled=True)
    gate = jax.nn.sigmoid(
        jnp.dot(gate_weight[layer], inputs, preferred_element_type=jnp.float32)
        + chan_bias[layer, 0][:, None]
    )
    if incoming:
        triangle = contract(left_cols, right_cols, 1, 1)
    else:
        triangle = contract(left_cols, right_cols, 2, 2)
    triangle_rows = lax.all_to_all(
        triangle.astype(jnp.bfloat16), "dap", split_axis=1, concat_axis=0, tiled=True
    )
    triangle_rows = triangle_rows.reshape(channels, rows * width)
    normed_tri, standard_out, inverse_out = normalize(
        triangle_rows.astype(jnp.float32), norm_gain[layer, 1], norm_shift[layer, 1]
    )
    tri_inputs = normed_tri.astype(jnp.bfloat16)
    linear = (
        jnp.dot(out_weight[layer], tri_inputs, preferred_element_type=jnp.float32)
        + chan_bias[layer, 1][:, None]
    )
    next_pair = (source + gate * linear).astype(jnp.bfloat16)
    saved = (
        inputs,
        standard_in,
        inverse_in,
        left_value,
        left_logit,
        right_value,
        right_logit,
        left_cols,
        right_cols,
        gate,
        linear,
        tri_inputs,
        standard_out,
        inverse_out,
    )
    return (next_pair, saved)


def backward_update(upstream, saved, params, layer, dims, incoming):
    proj_weight, proj_bias, gate_weight, out_weight, chan_bias, norm_gain, norm_shift = params
    channels, rows, width = dims
    (
        inputs,
        standard_in,
        inverse_in,
        left_value,
        left_logit,
        right_value,
        right_logit,
        left_cols,
        right_cols,
        gate,
        linear,
        tri_inputs,
        standard_out,
        inverse_out,
    ) = saved
    grad_linear = (upstream * gate).astype(jnp.bfloat16)
    grad_logit = (upstream * linear * gate * (1.0 - gate)).astype(jnp.bfloat16)
    grad_out_w = matmul_rows(grad_linear, tri_inputs)
    grad_out_b = jnp.sum(grad_linear.astype(jnp.float32), axis=1)
    grad_gate_w = matmul_rows(grad_logit, inputs)
    grad_gate_b = jnp.sum(grad_logit.astype(jnp.float32), axis=1)
    grad_normed = matmul_cols(out_weight[layer], grad_linear)
    grad_tri, gain_out, shift_out = normalize_back(
        grad_normed, norm_gain[layer, 1], standard_out, inverse_out
    )
    grad_cols = lax.all_to_all(
        grad_tri.astype(jnp.bfloat16).reshape(channels, rows, width),
        "dap",
        split_axis=0,
        concat_axis=1,
        tiled=True,
    )

    def left_term():
        if incoming:
            return contract(right_cols, grad_cols, 2, 2).astype(jnp.bfloat16)
        return contract(grad_cols, right_cols, 2, 1).astype(jnp.bfloat16)

    def right_term():
        if incoming:
            return contract(left_cols, grad_cols, 2, 1).astype(jnp.bfloat16)
        return contract(grad_cols, left_cols, 1, 1).astype(jnp.bfloat16)

    left_back = lax.all_to_all(left_term(), "dap", split_axis=1, concat_axis=0, tiled=True)
    right_back = lax.all_to_all(right_term(), "dap", split_axis=1, concat_axis=0, tiled=True)
    left_back = left_back.reshape(channels, rows * width).astype(jnp.float32)
    right_back = right_back.reshape(channels, rows * width).astype(jnp.float32)
    left_sig = jax.nn.sigmoid(left_logit)
    right_sig = jax.nn.sigmoid(right_logit)
    grad_pre = jnp.concatenate(
        [
            left_back * left_sig,
            left_back * left_value * left_sig * (1.0 - left_sig),
            right_back * right_sig,
            right_back * right_value * right_sig * (1.0 - right_sig),
        ],
        axis=0,
    ).astype(jnp.bfloat16)
    grad_proj_w = matmul_rows(grad_pre, inputs)
    grad_proj_b = jnp.sum(grad_pre.astype(jnp.float32), axis=1)
    grad_inputs = matmul_cols(proj_weight[layer], grad_pre) + matmul_cols(
        gate_weight[layer], grad_logit
    )
    grad_source, gain_in, shift_in = normalize_back(
        grad_inputs, norm_gain[layer, 0], standard_in, inverse_in
    )
    grads = (
        grad_proj_w,
        grad_proj_b,
        grad_gate_w,
        grad_out_w,
        jnp.stack([grad_gate_b, grad_out_b]),
        jnp.stack([gain_in, gain_out]),
        jnp.stack([shift_in, shift_out]),
    )
    return (upstream + grad_source, grads)


def large_body(
    pair,
    cotangent,
    proj_weight,
    proj_bias,
    gate_weight,
    out_weight,
    chan_bias,
    norm_gain,
    norm_shift,
):
    params = (proj_weight, proj_bias, gate_weight, out_weight, chan_bias, norm_gain, norm_shift)
    channels = pair.shape[1]
    rows = pair.shape[2]
    width = pair.shape[3]
    dims = (channels, rows, width)
    start_pair = pair[0].reshape(channels, rows * width)
    middle, saved_first = forward_update(start_pair, params, 0, dims, False)
    unused, saved_second = forward_update(middle, params, 1, dims, True)
    upstream = cotangent[0].reshape(channels, rows * width).astype(jnp.float32)
    grad_middle, grads_second = backward_update(upstream, saved_second, params, 1, dims, True)
    repeat_pair, saved_first = forward_update(start_pair, params, 0, dims, False)
    grad_start, grads_first = backward_update(grad_middle, saved_first, params, 0, dims, False)
    joined = tuple(
        (
            jnp.stack([first_part, second_part])
            for first_part, second_part in zip(grads_first, grads_second)
        )
    )
    stacked = lax.psum(
        (joined[0], joined[1], joined[2], joined[3], joined[4], joined[5], joined[6]), ("dap", "dp")
    )
    factor = 1.0 / width
    return (
        grad_start.astype(jnp.bfloat16).reshape(1, channels, rows, width),
        stacked[0] * factor,
        stacked[1] * factor,
        stacked[2] * factor,
        stacked[3] * factor,
        stacked[4] * factor,
        stacked[5] * factor,
        stacked[6] * factor,
    )


def norm_lanes(values, scale_by, offset):
    average = jnp.mean(values, axis=1, keepdims=True)
    centred = values - average
    variance = jnp.mean(centred * centred, axis=1, keepdims=True)
    inverse = lax.rsqrt(variance + EPSILON)
    standard = centred * inverse
    return (standard * scale_by + offset, standard, inverse)


def norm_lanes_back(upstream, scale_by, standard, inverse):
    scaled = upstream * scale_by
    adjusted = (
        scaled
        - jnp.mean(scaled, axis=1, keepdims=True)
        - standard * jnp.mean(scaled * standard, axis=1, keepdims=True)
    )
    return inverse * adjusted


def column_sum(values):
    return jnp.sum(values, axis=0, keepdims=True)


def rounded(values):
    return values.astype(jnp.bfloat16).astype(jnp.float32)


def products(width, a_ref, a_turned, b_ref, b_turned, o_ref):
    blocks = [
        b_ref[pl.ds(m, width, stride=width), :] if b_turned else b_ref[pl.ds(m * width, width), :]
        for m in range(width)
    ]

    def step(p, carry):
        total = None
        for m in range(width):
            row = a_ref[pl.ds(m * width + p if a_turned else p * width + m, 1), :]
            term = row * blocks[m]
            total = term if total is None else total + term
        o_ref[pl.ds(pl.multiple_of(p * width, width), width), :] = total
        return carry

    lax.fori_loop(0, width, step, 0)


def fused_kernel(
    peers,
    width,
    pair_hbm,
    cot_hbm,
    proj_hbm,
    gate_hbm,
    outw_hbm,
    bias_hbm,
    chan_hbm,
    gain_hbm,
    shift_hbm,
    dpair_out,
    big_out,
    dbias_out,
    dchan_out,
    dgain_out,
    dshift_out,
    dpair_ref,
    big_ref,
    dbias_ref,
    dchan_ref,
    dgain_ref,
    dshift_ref,
    proj_ref,
    gate_ref,
    outw_ref,
    bias_ref,
    chan_ref,
    gain_ref,
    shift_ref,
    pair_all,
    cot_all,
    left_s,
    right_s,
    tri_s,
    grad_s,
    dleft_s,
    dright_s,
    rows_s,
    send_half,
    recv_half,
    send_sum,
    recv_sum,
    small_all,
    fetch_done,
    store_done,
    gather_send,
    gather_recv,
    half_send,
    half_recv,
    sum_send,
    sum_recv,
    share_send,
    share_recv,
    small_send,
    small_recv,
):
    dap, dp = peers
    mesh_ids = pl.DeviceIdType.MESH
    held, channels = pair_hbm.shape
    me = lax.axis_index("dap")
    at = lax.axis_index("dp")
    core = lax.rem(at, 2)
    core_peer = at + 1 - 2 * core
    far_peer = lax.rem(at + 2, dp)

    own = pl.ds(pl.multiple_of(me * held, held), held)
    fetches = []
    for source, target in (
        (pair_hbm, pair_all.at[own]),
        (cot_hbm, cot_all.at[own]),
        (gain_hbm, gain_ref),
        (shift_hbm, shift_ref),
        (proj_hbm, proj_ref),
        (bias_hbm, bias_ref),
        (gate_hbm, gate_ref),
        (chan_hbm, chan_ref),
        (outw_hbm, outw_ref),
    ):
        copy = pltpu.make_async_copy(source, target, fetch_done.at[len(fetches)])
        copy.start()
        fetches.append(copy)

    barrier = pltpu.get_barrier_semaphore()
    for k in range(1, dap):
        pl.semaphore_signal(
            barrier, inc=1, device_id={"dap": lax.rem(me + k, dap)}, device_id_type=mesh_ids
        )
    for k in range(1, dp):
        pl.semaphore_signal(
            barrier, inc=1, device_id={"dp": lax.rem(at + k, dp)}, device_id_type=mesh_ids
        )
    pl.semaphore_wait(barrier, dap + dp - 2)

    gathers = []
    for slot, whole in enumerate((pair_all, cot_all)):
        fetches[slot].wait()
        copies = []
        for k in range(1, dap):
            copy = pltpu.make_async_remote_copy(
                src_ref=whole.at[own],
                dst_ref=whole.at[own],
                send_sem=gather_send.at[slot, k - 1],
                recv_sem=gather_recv.at[slot, k - 1],
                device_id={"dap": lax.rem(me + k, dap)},
                device_id_type=mesh_ids,
            )
            copy.start()
            copies.append(copy)
        gathers.append(copies)

    factor = 1.0 / width

    def forward(source, layer):
        normed, standard_in, inverse_in = norm_lanes(
            source, gain_ref[layer, 0:1, :], shift_ref[layer, 0:1, :]
        )
        inputs = normed.astype(jnp.bfloat16)
        pre_act = matmul_rows(inputs, proj_ref[layer]) + bias_ref[layer : layer + 1, :]
        left_value = pre_act[:, :channels]
        left_sig = jax.nn.sigmoid(pre_act[:, channels : 2 * channels])
        right_value = pre_act[:, 2 * channels : 3 * channels]
        right_sig = jax.nn.sigmoid(pre_act[:, 3 * channels :])
        left_s[layer] = rounded(left_sig * left_value)
        right_s[layer] = rounded(right_sig * right_value)
        gate = jax.nn.sigmoid(matmul_rows(inputs, gate_ref[layer]) + chan_ref[layer, 0:1, :])
        left, right = left_s.at[layer], right_s.at[layer]
        if layer == 0:
            products(width, left, False, right, True, tri_s)
        else:
            products(width, left, True, right, False, tri_s)
        normed_tri, standard_out, inverse_out = norm_lanes(
            rounded(tri_s[...]), gain_ref[layer, 1:2, :], shift_ref[layer, 1:2, :]
        )
        tri_inputs = normed_tri.astype(jnp.bfloat16)
        linear = matmul_rows(tri_inputs, outw_ref[layer]) + chan_ref[layer, 1:2, :]
        saved = (
            inputs,
            standard_in,
            inverse_in,
            left_value,
            left_sig,
            right_value,
            right_sig,
            gate,
            linear,
            tri_inputs,
            standard_out,
            inverse_out,
        )
        return saved

    def put_small(layer, row, values):
        rows_s[layer, row : row + 1, :] = values * factor

    def backward_near(upstream, saved, layer):
        inputs, _, _, _, _, _, _, gate, linear, tri_inputs, standard_out, inverse_out = saved
        grad_linear = (upstream * gate).astype(jnp.bfloat16)
        grad_logit = (upstream * linear * gate * (1.0 - gate)).astype(jnp.bfloat16)
        grad_normed = jnp.dot(grad_linear, outw_ref[layer], preferred_element_type=jnp.float32)
        grad_s[...] = rounded(
            norm_lanes_back(grad_normed, gain_ref[layer, 1:2, :], standard_out, inverse_out)
        )
        big_ref[layer, 4 * channels : 5 * channels, :] = matmul_cols(grad_logit, inputs) * factor
        big_ref[layer, 5 * channels :, :] = matmul_cols(grad_linear, tri_inputs) * factor
        put_small(layer, 4, column_sum(grad_logit.astype(jnp.float32)))
        put_small(layer, 5, column_sum(grad_linear.astype(jnp.float32)))
        put_small(layer, 7, column_sum(grad_normed * standard_out))
        put_small(layer, 9, column_sum(grad_normed))
        return grad_logit

    def backward_far(upstream, saved, grad_logit, layer):
        inputs, standard_in, inverse_in, left_value, left_sig, right_value, right_sig = saved[:7]
        left, right = left_s.at[layer], right_s.at[layer]
        if layer == 0:
            products(width, grad_s, False, right, False, dleft_s)
            products(width, grad_s, True, left, False, dright_s)
        else:
            products(width, right, False, grad_s, True, dleft_s)
            products(width, left, False, grad_s, False, dright_s)
        left_back = rounded(dleft_s[...])
        right_back = rounded(dright_s[...])
        blocks = (
            left_back * left_sig,
            left_back * left_value * left_sig * (1.0 - left_sig),
            right_back * right_sig,
            right_back * right_value * right_sig * (1.0 - right_sig),
        )
        grad_inputs = jnp.dot(grad_logit, gate_ref[layer], preferred_element_type=jnp.float32)
        for index, block in enumerate(blocks):
            part = block.astype(jnp.bfloat16)
            lines = slice(index * channels, (index + 1) * channels)
            big_ref[layer, lines, :] = matmul_cols(part, inputs) * factor
            put_small(layer, index, column_sum(part.astype(jnp.float32)))
            grad_inputs = grad_inputs + jnp.dot(
                part, proj_ref[layer, lines, :], preferred_element_type=jnp.float32
            )
        put_small(layer, 6, column_sum(grad_inputs * standard_in))
        put_small(layer, 8, column_sum(grad_inputs))
        return upstream + norm_lanes_back(
            grad_inputs, gain_ref[layer, 0:1, :], standard_in, inverse_in
        )

    pieces = (
        (1, 0, 6 * channels),
        (0, 4 * channels, 2 * channels),
        (0, 0, 4 * channels),
    )
    flights = {}
    stores = []

    def store(source, target):
        copy = pltpu.make_async_copy(source, target, store_done.at[len(stores)])
        copy.start()
        stores.append(copy)

    def spans(index):
        layer, first, count = pieces[index]
        half = count // 2
        mine = pl.ds(pl.multiple_of(first + core * half, half), half)
        other = pl.ds(pl.multiple_of(first + (1 - core) * half, half), half)
        slot = pl.ds(sum(piece[2] // 2 for piece in pieces[:index]), half)
        return (big_ref.at[layer], mine, other, slot)

    def exchange_half(index):
        whole, mine, other, slot = spans(index)
        send_half[slot, :] = whole[other, :].astype(jnp.bfloat16)
        copy = pltpu.make_async_remote_copy(
            src_ref=send_half.at[slot],
            dst_ref=recv_half.at[slot],
            send_sem=half_send.at[index],
            recv_sem=half_recv.at[index],
            device_id={"dp": core_peer},
            device_id_type=mesh_ids,
        )
        copy.start()
        flights[index] = [copy]

    def exchange_sum(index):
        whole, mine, other, slot = spans(index)
        flights[index][0].wait_recv()
        added = whole[mine, :] + recv_half[slot, :].astype(jnp.float32)
        send_sum[slot, :] = added.astype(jnp.bfloat16)
        copy = pltpu.make_async_remote_copy(
            src_ref=send_sum.at[slot],
            dst_ref=recv_sum.at[slot],
            send_sem=sum_send.at[index],
            recv_sem=sum_recv.at[index],
            device_id={"dp": far_peer},
            device_id_type=mesh_ids,
        )
        copy.start()
        flights[index].append(copy)

    def share(index):
        whole, mine, other, slot = spans(index)
        flights[index][1].wait_recv()
        whole[mine, :] = send_sum[slot, :].astype(jnp.float32) + recv_sum[slot, :].astype(
            jnp.float32
        )
        copy = pltpu.make_async_remote_copy(
            src_ref=whole.at[mine],
            dst_ref=big_out.at[pieces[index][0], mine],
            send_sem=share_send.at[index],
            recv_sem=share_recv.at[index],
            device_id={"dp": core_peer},
            device_id_type=mesh_ids,
        )
        copy.start()
        flights[index].append(copy)
        store(whole.at[mine], big_out.at[pieces[index][0], mine])

    for copy in fetches[2:]:
        copy.wait()
    for copy in gathers[0]:
        copy.wait_recv()
    start_pair = pair_all[...].astype(jnp.float32)
    saved_first = forward(start_pair, 0)
    middle = rounded(start_pair + saved_first[7] * saved_first[8])
    saved_second = forward(middle, 1)
    for copy in gathers[1]:
        copy.wait_recv()
    upstream = cot_all[...].astype(jnp.float32)
    grad_logit = backward_near(upstream, saved_second, 1)
    grad_middle = backward_far(upstream, saved_second, grad_logit, 1)
    exchange_half(0)
    grad_logit = backward_near(grad_middle, saved_first, 0)
    exchange_half(1)
    exchange_sum(0)
    grad_start = backward_far(grad_middle, saved_first, grad_logit, 0)
    exchange_half(2)
    small_all[at] = rows_s[...]
    small_copies = []
    for k in range(1, dp):
        copy = pltpu.make_async_remote_copy(
            src_ref=rows_s,
            dst_ref=small_all.at[at],
            send_sem=small_send.at[k - 1],
            recv_sem=small_recv.at[k - 1],
            device_id={"dp": lax.rem(at + k, dp)},
            device_id_type=mesh_ids,
        )
        copy.start()
        small_copies.append(copy)
    exchange_sum(1)
    exchange_sum(2)
    dleft_s[...] = grad_start
    dpair_ref[...] = dleft_s[own, :].astype(jnp.bfloat16)
    store(dpair_ref, dpair_out)
    share(0)
    share(1)
    for copy in small_copies:
        copy.wait_recv()
    total = small_all[0]
    for index in range(1, dp):
        total = total + small_all[index]
    for index in range(4):
        dbias_ref[:, index * channels : (index + 1) * channels] = total[:, index]
    dchan_ref[...] = total[:, 4:6]
    dgain_ref[...] = total[:, 6:8]
    dshift_ref[...] = total[:, 8:10]
    store(dbias_ref, dbias_out)
    store(dchan_ref, dchan_out)
    store(dgain_ref, dgain_out)
    store(dshift_ref, dshift_out)
    share(2)
    for index in range(3):
        flights[index][2].wait_recv()
    for index in range(3):
        for copy in flights[index]:
            copy.wait_send()
    for copy in gathers[0] + gathers[1] + small_copies:
        copy.wait_send()
    for copy in stores:
        copy.wait()


def deliver_kernel(
    dpair_ref,
    big_ref,
    dbias_ref,
    dchan_ref,
    dgain_ref,
    dshift_ref,
    dpair_out,
    proj_out,
    bias_out,
    gate_out,
    outw_out,
    chan_out,
    gain_out,
    shift_out,
    done,
):
    channels = big_ref.shape[2]
    copies = []
    for source, target in (
        (big_ref.at[:, : 4 * channels], proj_out),
        (big_ref.at[:, 4 * channels : 5 * channels], gate_out),
        (big_ref.at[:, 5 * channels :], outw_out),
        (dpair_ref, dpair_out),
        (dbias_ref, bias_out),
        (dchan_ref, chan_out),
        (dgain_ref, gain_out),
        (dshift_ref, shift_out),
    ):
        copy = pltpu.make_async_copy(source, target, done.at[len(copies)])
        copy.start()
        copies.append(copy)
    for copy in copies:
        copy.wait()


def fused_body(
    peers,
    pair,
    cotangent,
    proj_weight,
    proj_bias,
    gate_weight,
    out_weight,
    chan_bias,
    norm_gain,
    norm_shift,
):
    dap, dp = peers
    _, channels, rows, width = pair.shape
    held = rows * width
    entries = width * width
    float_rows = pltpu.VMEM((entries, channels), jnp.float32)
    layer_rows = pltpu.VMEM((2, entries, channels), jnp.float32)
    half_rows = pltpu.VMEM((6 * channels, channels), jnp.bfloat16)
    hbm = pl.BlockSpec(memory_space=pltpu.HBM)
    summed = pl.pallas_call(
        functools.partial(fused_kernel, peers, width),
        out_shape=(
            jax.ShapeDtypeStruct((held, channels), jnp.bfloat16),
            jax.ShapeDtypeStruct((2, 6 * channels, channels), jnp.float32),
            jax.ShapeDtypeStruct((2, 4 * channels), jnp.float32),
            jax.ShapeDtypeStruct((2, 2, channels), jnp.float32),
            jax.ShapeDtypeStruct((2, 2, channels), jnp.float32),
            jax.ShapeDtypeStruct((2, 2, channels), jnp.float32),
        ),
        in_specs=[hbm] * 9,
        out_specs=(hbm,) * 6,
        scratch_shapes=[
            pltpu.VMEM((held, channels), jnp.bfloat16),
            pltpu.VMEM((2, 6 * channels, channels), jnp.float32),
            pltpu.VMEM((2, 4 * channels), jnp.float32),
            pltpu.VMEM((2, 2, channels), jnp.float32),
            pltpu.VMEM((2, 2, channels), jnp.float32),
            pltpu.VMEM((2, 2, channels), jnp.float32),
            pltpu.VMEM(proj_weight.shape, jnp.bfloat16),
            pltpu.VMEM(gate_weight.shape, jnp.bfloat16),
            pltpu.VMEM(out_weight.shape, jnp.bfloat16),
            pltpu.VMEM(proj_bias.shape, jnp.float32),
            pltpu.VMEM(chan_bias.shape, jnp.float32),
            pltpu.VMEM(norm_gain.shape, jnp.float32),
            pltpu.VMEM(norm_shift.shape, jnp.float32),
            pltpu.VMEM((entries, channels), jnp.bfloat16),
            pltpu.VMEM((entries, channels), jnp.bfloat16),
            layer_rows,
            layer_rows,
            float_rows,
            float_rows,
            float_rows,
            float_rows,
            pltpu.VMEM((2, 10, channels), jnp.float32),
            half_rows,
            half_rows,
            half_rows,
            half_rows,
            pltpu.VMEM((dp, 2, 10, channels), jnp.float32),
            pltpu.SemaphoreType.DMA((9,)),
            pltpu.SemaphoreType.DMA((8,)),
            pltpu.SemaphoreType.DMA((2, dap - 1)),
            pltpu.SemaphoreType.DMA((2, dap - 1)),
            pltpu.SemaphoreType.DMA((3,)),
            pltpu.SemaphoreType.DMA((3,)),
            pltpu.SemaphoreType.DMA((3,)),
            pltpu.SemaphoreType.DMA((3,)),
            pltpu.SemaphoreType.DMA((3,)),
            pltpu.SemaphoreType.DMA((3,)),
            pltpu.SemaphoreType.DMA((dp - 1,)),
            pltpu.SemaphoreType.DMA((dp - 1,)),
        ],
        compiler_params=pltpu.CompilerParams(
            collective_id=0, has_side_effects=True, vmem_limit_bytes=62 * 1024 * 1024
        ),
        name="triangle_updates",
    )(
        pair[0].reshape(channels, held).T,
        cotangent[0].reshape(channels, held).T,
        proj_weight,
        gate_weight,
        out_weight,
        proj_bias,
        chan_bias,
        norm_gain,
        norm_shift,
    )
    outputs = pl.pallas_call(
        deliver_kernel,
        out_shape=(
            jax.ShapeDtypeStruct((held, channels), jnp.bfloat16),
            jax.ShapeDtypeStruct((2, 4 * channels, channels), jnp.float32),
            jax.ShapeDtypeStruct((2, 4 * channels), jnp.float32),
            jax.ShapeDtypeStruct((2, channels, channels), jnp.float32),
            jax.ShapeDtypeStruct((2, channels, channels), jnp.float32),
            jax.ShapeDtypeStruct((2, 2, channels), jnp.float32),
            jax.ShapeDtypeStruct((2, 2, channels), jnp.float32),
            jax.ShapeDtypeStruct((2, 2, channels), jnp.float32),
        ),
        in_specs=[hbm] * 6,
        out_specs=(hbm,) * 8,
        scratch_shapes=[pltpu.SemaphoreType.DMA((8,))],
        compiler_params=pltpu.CompilerParams(vmem_limit_bytes=62 * 1024 * 1024),
        name="deliver",
    )(*summed)
    return (outputs[0].T.reshape(1, channels, rows, width),) + tuple(outputs[1:])


def any_body(peers, pair, *others):
    _, channels, rows, width = pair.shape
    small = channels == 128 and width == 16 and rows % 4 == 0
    if small and peers[1] == 4 and peers[0] > 1:
        return fused_body(peers, pair, *others)
    return large_body(pair, *others)


def solution(mesh):
    in_specs = (
        P(("groups", "dp"), None, "dap", None),
        P(("groups", "dp"), None, "dap", None),
        P(),
        P(),
        P(),
        P(),
        P(),
        P(),
        P(),
    )
    out_specs = (
        P(("groups", "dp"), None, "dap", None),
        P("groups", None, None),
        P("groups", None),
        P("groups", None, None),
        P("groups", None, None),
        P("groups", None, None),
        P("groups", None, None),
        P("groups", None, None),
    )
    peers = (mesh.shape["dap"], mesh.shape["dp"])
    body = functools.partial(any_body, peers)
    return jax.shard_map(body, mesh=mesh, in_specs=in_specs, out_specs=out_specs, check_vma=False)
```

```python
import functools

import jax
import jax.numpy as jnp
from jax import lax
from jax.experimental import pallas as pl
from jax.experimental.pallas import tpu as pltpu
from jax.sharding import PartitionSpec as P

EPSILON = 1e-05


def normalize(values, scale_by, offset):
    average = jnp.mean(values, axis=0, keepdims=True)
    centred = values - average
    variance = jnp.mean(centred * centred, axis=0, keepdims=True)
    inverse = lax.rsqrt(variance + EPSILON)
    standard = centred * inverse
    return (standard * scale_by[:, None] + offset[:, None], standard, inverse)


def normalize_back(upstream, scale_by, standard, inverse):
    scaled = upstream * scale_by[:, None]
    adjusted = (
        scaled
        - jnp.mean(scaled, axis=0, keepdims=True)
        - standard * jnp.mean(scaled * standard, axis=0, keepdims=True)
    )
    return (inverse * adjusted, jnp.sum(upstream * standard, axis=1), jnp.sum(upstream, axis=1))


def matmul_rows(left, right):
    return lax.dot_general(
        left, right, (((1,), (1,)), ((), ())), preferred_element_type=jnp.float32
    )


def matmul_cols(left, right):
    return lax.dot_general(
        left, right, (((0,), (0,)), ((), ())), preferred_element_type=jnp.float32
    )


def contract(left, right, left_dim, right_dim):
    return lax.dot_general(
        left, right, (((left_dim,), (right_dim,)), ((0,), (0,))), preferred_element_type=jnp.float32
    )


def forward_update(pair_rows, params, layer, dims, incoming):
    proj_weight, proj_bias, gate_weight, out_weight, chan_bias, norm_gain, norm_shift = params
    channels, rows, width = dims
    source = pair_rows.astype(jnp.float32)
    normed, standard_in, inverse_in = normalize(source, norm_gain[layer, 0], norm_shift[layer, 0])
    inputs = normed.astype(jnp.bfloat16)
    weight_now = proj_weight[layer]
    bias_now = proj_bias[layer]

    def gated(first_row):
        pre_act = jnp.dot(
            weight_now[first_row : first_row + 2 * channels],
            inputs,
            preferred_element_type=jnp.float32,
        )
        pre_act = pre_act + bias_now[first_row : first_row + 2 * channels][:, None]
        value = pre_act[:channels]
        logit = pre_act[channels:]
        product = (
            (jax.nn.sigmoid(logit) * value).astype(jnp.bfloat16).reshape(channels, rows, width)
        )
        return (product, value, logit)

    left_rows, left_value, left_logit = gated(0)
    left_cols = lax.all_to_all(left_rows, "dap", split_axis=0, concat_axis=1, tiled=True)
    right_rows, right_value, right_logit = gated(2 * channels)
    right_cols = lax.all_to_all(right_rows, "dap", split_axis=0, concat_axis=1, tiled=True)
    gate = jax.nn.sigmoid(
        jnp.dot(gate_weight[layer], inputs, preferred_element_type=jnp.float32)
        + chan_bias[layer, 0][:, None]
    )
    if incoming:
        triangle = contract(left_cols, right_cols, 1, 1)
    else:
        triangle = contract(left_cols, right_cols, 2, 2)
    triangle_rows = lax.all_to_all(
        triangle.astype(jnp.bfloat16), "dap", split_axis=1, concat_axis=0, tiled=True
    )
    triangle_rows = triangle_rows.reshape(channels, rows * width)
    normed_tri, standard_out, inverse_out = normalize(
        triangle_rows.astype(jnp.float32), norm_gain[layer, 1], norm_shift[layer, 1]
    )
    tri_inputs = normed_tri.astype(jnp.bfloat16)
    linear = (
        jnp.dot(out_weight[layer], tri_inputs, preferred_element_type=jnp.float32)
        + chan_bias[layer, 1][:, None]
    )
    next_pair = (source + gate * linear).astype(jnp.bfloat16)
    saved = (
        inputs,
        standard_in,
        inverse_in,
        left_value,
        left_logit,
        right_value,
        right_logit,
        left_cols,
        right_cols,
        gate,
        linear,
        tri_inputs,
        standard_out,
        inverse_out,
    )
    return (next_pair, saved)


def backward_update(upstream, saved, params, layer, dims, incoming):
    proj_weight, proj_bias, gate_weight, out_weight, chan_bias, norm_gain, norm_shift = params
    channels, rows, width = dims
    (
        inputs,
        standard_in,
        inverse_in,
        left_value,
        left_logit,
        right_value,
        right_logit,
        left_cols,
        right_cols,
        gate,
        linear,
        tri_inputs,
        standard_out,
        inverse_out,
    ) = saved
    grad_linear = (upstream * gate).astype(jnp.bfloat16)
    grad_logit = (upstream * linear * gate * (1.0 - gate)).astype(jnp.bfloat16)
    grad_out_w = matmul_rows(grad_linear, tri_inputs)
    grad_out_b = jnp.sum(grad_linear.astype(jnp.float32), axis=1)
    grad_gate_w = matmul_rows(grad_logit, inputs)
    grad_gate_b = jnp.sum(grad_logit.astype(jnp.float32), axis=1)
    grad_normed = matmul_cols(out_weight[layer], grad_linear)
    grad_tri, gain_out, shift_out = normalize_back(
        grad_normed, norm_gain[layer, 1], standard_out, inverse_out
    )
    grad_cols = lax.all_to_all(
        grad_tri.astype(jnp.bfloat16).reshape(channels, rows, width),
        "dap",
        split_axis=0,
        concat_axis=1,
        tiled=True,
    )

    def left_term():
        if incoming:
            return contract(right_cols, grad_cols, 2, 2).astype(jnp.bfloat16)
        return contract(grad_cols, right_cols, 2, 1).astype(jnp.bfloat16)

    def right_term():
        if incoming:
            return contract(left_cols, grad_cols, 2, 1).astype(jnp.bfloat16)
        return contract(grad_cols, left_cols, 1, 1).astype(jnp.bfloat16)

    left_back = lax.all_to_all(left_term(), "dap", split_axis=1, concat_axis=0, tiled=True)
    right_back = lax.all_to_all(right_term(), "dap", split_axis=1, concat_axis=0, tiled=True)
    left_back = left_back.reshape(channels, rows * width).astype(jnp.float32)
    right_back = right_back.reshape(channels, rows * width).astype(jnp.float32)
    left_sig = jax.nn.sigmoid(left_logit)
    right_sig = jax.nn.sigmoid(right_logit)
    grad_pre = jnp.concatenate(
        [
            left_back * left_sig,
            left_back * left_value * left_sig * (1.0 - left_sig),
            right_back * right_sig,
            right_back * right_value * right_sig * (1.0 - right_sig),
        ],
        axis=0,
    ).astype(jnp.bfloat16)
    grad_proj_w = matmul_rows(grad_pre, inputs)
    grad_proj_b = jnp.sum(grad_pre.astype(jnp.float32), axis=1)
    grad_inputs = matmul_cols(proj_weight[layer], grad_pre) + matmul_cols(
        gate_weight[layer], grad_logit
    )
    grad_source, gain_in, shift_in = normalize_back(
        grad_inputs, norm_gain[layer, 0], standard_in, inverse_in
    )
    grads = (
        grad_proj_w,
        grad_proj_b,
        grad_gate_w,
        grad_out_w,
        jnp.stack([grad_gate_b, grad_out_b]),
        jnp.stack([gain_in, gain_out]),
        jnp.stack([shift_in, shift_out]),
    )
    return (upstream + grad_source, grads)


def large_body(
    pair,
    cotangent,
    proj_weight,
    proj_bias,
    gate_weight,
    out_weight,
    chan_bias,
    norm_gain,
    norm_shift,
):
    params = (proj_weight, proj_bias, gate_weight, out_weight, chan_bias, norm_gain, norm_shift)
    channels = pair.shape[1]
    rows = pair.shape[2]
    width = pair.shape[3]
    dims = (channels, rows, width)
    start_pair = pair[0].reshape(channels, rows * width)
    middle, saved_first = forward_update(start_pair, params, 0, dims, False)
    unused, saved_second = forward_update(middle, params, 1, dims, True)
    upstream = cotangent[0].reshape(channels, rows * width).astype(jnp.float32)
    grad_middle, grads_second = backward_update(upstream, saved_second, params, 1, dims, True)
    repeat_pair, saved_first = forward_update(start_pair, params, 0, dims, False)
    grad_start, grads_first = backward_update(grad_middle, saved_first, params, 0, dims, False)
    joined = tuple(
        (
            jnp.stack([first_part, second_part])
            for first_part, second_part in zip(grads_first, grads_second)
        )
    )
    stacked = lax.psum(
        (joined[0], joined[1], joined[2], joined[3], joined[4], joined[5], joined[6]), ("dap", "dp")
    )
    factor = 1.0 / width
    return (
        grad_start.astype(jnp.bfloat16).reshape(1, channels, rows, width),
        stacked[0] * factor,
        stacked[1] * factor,
        stacked[2] * factor,
        stacked[3] * factor,
        stacked[4] * factor,
        stacked[5] * factor,
        stacked[6] * factor,
    )


def norm_lanes(values, scale_by, offset):
    average = jnp.mean(values, axis=1, keepdims=True)
    centred = values - average
    variance = jnp.mean(centred * centred, axis=1, keepdims=True)
    inverse = lax.rsqrt(variance + EPSILON)
    standard = centred * inverse
    return (standard * scale_by + offset, standard, inverse)


def norm_lanes_back(upstream, scale_by, standard, inverse):
    scaled = upstream * scale_by
    adjusted = (
        scaled
        - jnp.mean(scaled, axis=1, keepdims=True)
        - standard * jnp.mean(scaled * standard, axis=1, keepdims=True)
    )
    return inverse * adjusted


def column_sum(values):
    return jnp.sum(values, axis=0, keepdims=True)


def rounded(values):
    return values.astype(jnp.bfloat16).astype(jnp.float32)


def products(width, a_ref, a_turned, b_ref, b_turned, o_ref):
    blocks = [
        b_ref[pl.ds(m, width, stride=width), :] if b_turned else b_ref[pl.ds(m * width, width), :]
        for m in range(width)
    ]

    def step(p, carry):
        total = None
        for m in range(width):
            row = a_ref[pl.ds(m * width + p if a_turned else p * width + m, 1), :]
            term = row * blocks[m]
            total = term if total is None else total + term
        o_ref[pl.ds(pl.multiple_of(p * width, width), width), :] = total
        return carry

    lax.fori_loop(0, width, step, 0)


def fused_kernel(
    peers,
    width,
    pair_hbm,
    cot_hbm,
    proj_hbm,
    gate_hbm,
    outw_hbm,
    bias_hbm,
    chan_hbm,
    gain_hbm,
    shift_hbm,
    dpair_ref,
    big_ref,
    dbias_ref,
    dchan_ref,
    dgain_ref,
    dshift_ref,
    proj_ref,
    gate_ref,
    outw_ref,
    bias_ref,
    chan_ref,
    gain_ref,
    shift_ref,
    pair_all,
    cot_all,
    left_s,
    right_s,
    tri_s,
    grad_s,
    dleft_s,
    dright_s,
    rows_s,
    send_half,
    recv_half,
    send_sum,
    recv_sum,
    small_all,
    fetch_done,
    gather_send,
    gather_recv,
    half_send,
    half_recv,
    sum_send,
    sum_recv,
    share_send,
    share_recv,
    small_send,
    small_recv,
):
    dap, dp = peers
    mesh_ids = pl.DeviceIdType.MESH
    held, channels = pair_hbm.shape
    me = lax.axis_index("dap")
    at = lax.axis_index("dp")
    core = lax.rem(at, 2)
    core_peer = at + 1 - 2 * core
    far_peer = lax.rem(at + 2, dp)

    own = pl.ds(pl.multiple_of(me * held, held), held)
    fetches = []
    for source, target in (
        (pair_hbm, pair_all.at[own]),
        (cot_hbm, cot_all.at[own]),
        (gain_hbm, gain_ref),
        (shift_hbm, shift_ref),
        (proj_hbm, proj_ref),
        (bias_hbm, bias_ref),
        (gate_hbm, gate_ref),
        (chan_hbm, chan_ref),
        (outw_hbm, outw_ref),
    ):
        copy = pltpu.make_async_copy(source, target, fetch_done.at[len(fetches)])
        copy.start()
        fetches.append(copy)

    barrier = pltpu.get_barrier_semaphore()
    for k in range(1, dap):
        pl.semaphore_signal(
            barrier, inc=1, device_id={"dap": lax.rem(me + k, dap)}, device_id_type=mesh_ids
        )
    for k in range(1, dp):
        pl.semaphore_signal(
            barrier, inc=1, device_id={"dp": lax.rem(at + k, dp)}, device_id_type=mesh_ids
        )
    pl.semaphore_wait(barrier, dap + dp - 2)

    gathers = []
    for slot, whole in enumerate((pair_all, cot_all)):
        fetches[slot].wait()
        copies = []
        for k in range(1, dap):
            copy = pltpu.make_async_remote_copy(
                src_ref=whole.at[own],
                dst_ref=whole.at[own],
                send_sem=gather_send.at[slot, k - 1],
                recv_sem=gather_recv.at[slot, k - 1],
                device_id={"dap": lax.rem(me + k, dap)},
                device_id_type=mesh_ids,
            )
            copy.start()
            copies.append(copy)
        gathers.append(copies)

    factor = 1.0 / width

    def forward(source, layer):
        normed, standard_in, inverse_in = norm_lanes(
            source, gain_ref[layer, 0:1, :], shift_ref[layer, 0:1, :]
        )
        inputs = normed.astype(jnp.bfloat16)
        pre_act = matmul_rows(inputs, proj_ref[layer]) + bias_ref[layer : layer + 1, :]
        left_value = pre_act[:, :channels]
        left_sig = jax.nn.sigmoid(pre_act[:, channels : 2 * channels])
        right_value = pre_act[:, 2 * channels : 3 * channels]
        right_sig = jax.nn.sigmoid(pre_act[:, 3 * channels :])
        left_s[layer] = rounded(left_sig * left_value)
        right_s[layer] = rounded(right_sig * right_value)
        gate = jax.nn.sigmoid(matmul_rows(inputs, gate_ref[layer]) + chan_ref[layer, 0:1, :])
        left, right = left_s.at[layer], right_s.at[layer]
        if layer == 0:
            products(width, left, False, right, True, tri_s)
        else:
            products(width, left, True, right, False, tri_s)
        normed_tri, standard_out, inverse_out = norm_lanes(
            rounded(tri_s[...]), gain_ref[layer, 1:2, :], shift_ref[layer, 1:2, :]
        )
        tri_inputs = normed_tri.astype(jnp.bfloat16)
        linear = matmul_rows(tri_inputs, outw_ref[layer]) + chan_ref[layer, 1:2, :]
        saved = (
            inputs,
            standard_in,
            inverse_in,
            left_value,
            left_sig,
            right_value,
            right_sig,
            gate,
            linear,
            tri_inputs,
            standard_out,
            inverse_out,
        )
        return saved

    def put_small(layer, row, values):
        rows_s[layer, row : row + 1, :] = values * factor

    def backward_near(upstream, saved, layer):
        inputs, _, _, _, _, _, _, gate, linear, tri_inputs, standard_out, inverse_out = saved
        grad_linear = (upstream * gate).astype(jnp.bfloat16)
        grad_logit = (upstream * linear * gate * (1.0 - gate)).astype(jnp.bfloat16)
        grad_normed = jnp.dot(grad_linear, outw_ref[layer], preferred_element_type=jnp.float32)
        grad_s[...] = rounded(
            norm_lanes_back(grad_normed, gain_ref[layer, 1:2, :], standard_out, inverse_out)
        )
        big_ref[layer, 4 * channels : 5 * channels, :] = matmul_cols(grad_logit, inputs) * factor
        big_ref[layer, 5 * channels :, :] = matmul_cols(grad_linear, tri_inputs) * factor
        put_small(layer, 4, column_sum(grad_logit.astype(jnp.float32)))
        put_small(layer, 5, column_sum(grad_linear.astype(jnp.float32)))
        put_small(layer, 7, column_sum(grad_normed * standard_out))
        put_small(layer, 9, column_sum(grad_normed))
        return grad_logit

    def backward_far(upstream, saved, grad_logit, layer):
        inputs, standard_in, inverse_in, left_value, left_sig, right_value, right_sig = saved[:7]
        left, right = left_s.at[layer], right_s.at[layer]
        if layer == 0:
            products(width, grad_s, False, right, False, dleft_s)
            products(width, grad_s, True, left, False, dright_s)
        else:
            products(width, right, False, grad_s, True, dleft_s)
            products(width, left, False, grad_s, False, dright_s)
        left_back = rounded(dleft_s[...])
        right_back = rounded(dright_s[...])
        blocks = (
            left_back * left_sig,
            left_back * left_value * left_sig * (1.0 - left_sig),
            right_back * right_sig,
            right_back * right_value * right_sig * (1.0 - right_sig),
        )
        grad_inputs = jnp.dot(grad_logit, gate_ref[layer], preferred_element_type=jnp.float32)
        for index, block in enumerate(blocks):
            part = block.astype(jnp.bfloat16)
            lines = slice(index * channels, (index + 1) * channels)
            big_ref[layer, lines, :] = matmul_cols(part, inputs) * factor
            put_small(layer, index, column_sum(part.astype(jnp.float32)))
            grad_inputs = grad_inputs + jnp.dot(
                part, proj_ref[layer, lines, :], preferred_element_type=jnp.float32
            )
        put_small(layer, 6, column_sum(grad_inputs * standard_in))
        put_small(layer, 8, column_sum(grad_inputs))
        return upstream + norm_lanes_back(
            grad_inputs, gain_ref[layer, 0:1, :], standard_in, inverse_in
        )

    pieces = (
        (1, 0, 6 * channels),
        (0, 4 * channels, 2 * channels),
        (0, 0, 4 * channels),
    )
    flights = {}

    def spans(index):
        layer, first, count = pieces[index]
        half = count // 2
        mine = pl.ds(pl.multiple_of(first + core * half, half), half)
        other = pl.ds(pl.multiple_of(first + (1 - core) * half, half), half)
        slot = pl.ds(sum(piece[2] // 2 for piece in pieces[:index]), half)
        return (big_ref.at[layer], mine, other, slot)

    def exchange_half(index):
        whole, mine, other, slot = spans(index)
        send_half[slot, :] = whole[other, :].astype(jnp.bfloat16)
        copy = pltpu.make_async_remote_copy(
            src_ref=send_half.at[slot],
            dst_ref=recv_half.at[slot],
            send_sem=half_send.at[index],
            recv_sem=half_recv.at[index],
            device_id={"dp": core_peer},
            device_id_type=mesh_ids,
        )
        copy.start()
        flights[index] = [copy]

    def exchange_sum(index):
        whole, mine, other, slot = spans(index)
        flights[index][0].wait_recv()
        added = whole[mine, :] + recv_half[slot, :].astype(jnp.float32)
        send_sum[slot, :] = added.astype(jnp.bfloat16)
        copy = pltpu.make_async_remote_copy(
            src_ref=send_sum.at[slot],
            dst_ref=recv_sum.at[slot],
            send_sem=sum_send.at[index],
            recv_sem=sum_recv.at[index],
            device_id={"dp": far_peer},
            device_id_type=mesh_ids,
        )
        copy.start()
        flights[index].append(copy)

    def share(index):
        whole, mine, other, slot = spans(index)
        flights[index][1].wait_recv()
        whole[mine, :] = send_sum[slot, :].astype(jnp.float32) + recv_sum[slot, :].astype(
            jnp.float32
        )
        copy = pltpu.make_async_remote_copy(
            src_ref=whole.at[mine],
            dst_ref=whole.at[mine],
            send_sem=share_send.at[index],
            recv_sem=share_recv.at[index],
            device_id={"dp": core_peer},
            device_id_type=mesh_ids,
        )
        copy.start()
        flights[index].append(copy)

    for copy in fetches[2:]:
        copy.wait()
    for copy in gathers[0]:
        copy.wait_recv()
    start_pair = pair_all[...].astype(jnp.float32)
    saved_first = forward(start_pair, 0)
    middle = rounded(start_pair + saved_first[7] * saved_first[8])
    saved_second = forward(middle, 1)
    for copy in gathers[1]:
        copy.wait_recv()
    upstream = cot_all[...].astype(jnp.float32)
    grad_logit = backward_near(upstream, saved_second, 1)
    grad_middle = backward_far(upstream, saved_second, grad_logit, 1)
    exchange_half(0)
    grad_logit = backward_near(grad_middle, saved_first, 0)
    exchange_half(1)
    exchange_sum(0)
    grad_start = backward_far(grad_middle, saved_first, grad_logit, 0)
    exchange_half(2)
    small_all[at] = rows_s[...]
    small_copies = []
    for k in range(1, dp):
        copy = pltpu.make_async_remote_copy(
            src_ref=rows_s,
            dst_ref=small_all.at[at],
            send_sem=small_send.at[k - 1],
            recv_sem=small_recv.at[k - 1],
            device_id={"dp": lax.rem(at + k, dp)},
            device_id_type=mesh_ids,
        )
        copy.start()
        small_copies.append(copy)
    exchange_sum(1)
    exchange_sum(2)
    dleft_s[...] = grad_start
    dpair_ref[...] = dleft_s[own, :].astype(jnp.bfloat16)
    share(0)
    share(1)
    for copy in small_copies:
        copy.wait_recv()
    total = small_all[0]
    for index in range(1, dp):
        total = total + small_all[index]
    for index in range(4):
        dbias_ref[:, index * channels : (index + 1) * channels] = total[:, index]
    dchan_ref[...] = total[:, 4:6]
    dgain_ref[...] = total[:, 6:8]
    dshift_ref[...] = total[:, 8:10]
    share(2)
    for index in range(3):
        flights[index][2].wait_recv()
    for index in range(3):
        for copy in flights[index]:
            copy.wait_send()
    for copy in gathers[0] + gathers[1] + small_copies:
        copy.wait_send()


def deliver_kernel(
    dpair_ref,
    big_ref,
    dbias_ref,
    dchan_ref,
    dgain_ref,
    dshift_ref,
    dpair_out,
    proj_out,
    bias_out,
    gate_out,
    outw_out,
    chan_out,
    gain_out,
    shift_out,
    done,
):
    channels = big_ref.shape[2]
    copies = []
    for source, target in (
        (big_ref.at[:, : 4 * channels], proj_out),
        (big_ref.at[:, 4 * channels : 5 * channels], gate_out),
        (big_ref.at[:, 5 * channels :], outw_out),
        (dpair_ref, dpair_out),
        (dbias_ref, bias_out),
        (dchan_ref, chan_out),
        (dgain_ref, gain_out),
        (dshift_ref, shift_out),
    ):
        copy = pltpu.make_async_copy(source, target, done.at[len(copies)])
        copy.start()
        copies.append(copy)
    for copy in copies:
        copy.wait()


def fused_body(
    peers,
    pair,
    cotangent,
    proj_weight,
    proj_bias,
    gate_weight,
    out_weight,
    chan_bias,
    norm_gain,
    norm_shift,
):
    dap, dp = peers
    _, channels, rows, width = pair.shape
    held = rows * width
    entries = width * width
    float_rows = pltpu.VMEM((entries, channels), jnp.float32)
    layer_rows = pltpu.VMEM((2, entries, channels), jnp.float32)
    half_rows = pltpu.VMEM((6 * channels, channels), jnp.bfloat16)
    vmem = pl.BlockSpec(memory_space=pltpu.VMEM)
    hbm = pl.BlockSpec(memory_space=pltpu.HBM)
    summed = pl.pallas_call(
        functools.partial(fused_kernel, peers, width),
        out_shape=(
            pltpu.VMEM((held, channels), jnp.bfloat16),
            pltpu.VMEM((2, 6 * channels, channels), jnp.float32),
            pltpu.VMEM((2, 4 * channels), jnp.float32),
            pltpu.VMEM((2, 2, channels), jnp.float32),
            pltpu.VMEM((2, 2, channels), jnp.float32),
            pltpu.VMEM((2, 2, channels), jnp.float32),
        ),
        in_specs=[hbm] * 9,
        out_specs=(vmem,) * 6,
        scratch_shapes=[
            pltpu.VMEM(proj_weight.shape, jnp.bfloat16),
            pltpu.VMEM(gate_weight.shape, jnp.bfloat16),
            pltpu.VMEM(out_weight.shape, jnp.bfloat16),
            pltpu.VMEM(proj_bias.shape, jnp.float32),
            pltpu.VMEM(chan_bias.shape, jnp.float32),
            pltpu.VMEM(norm_gain.shape, jnp.float32),
            pltpu.VMEM(norm_shift.shape, jnp.float32),
            pltpu.VMEM((entries, channels), jnp.bfloat16),
            pltpu.VMEM((entries, channels), jnp.bfloat16),
            layer_rows,
            layer_rows,
            float_rows,
            float_rows,
            float_rows,
            float_rows,
            pltpu.VMEM((2, 10, channels), jnp.float32),
            half_rows,
            half_rows,
            half_rows,
            half_rows,
            pltpu.VMEM((dp, 2, 10, channels), jnp.float32),
            pltpu.SemaphoreType.DMA((9,)),
            pltpu.SemaphoreType.DMA((2, dap - 1)),
            pltpu.SemaphoreType.DMA((2, dap - 1)),
            pltpu.SemaphoreType.DMA((3,)),
            pltpu.SemaphoreType.DMA((3,)),
            pltpu.SemaphoreType.DMA((3,)),
            pltpu.SemaphoreType.DMA((3,)),
            pltpu.SemaphoreType.DMA((3,)),
            pltpu.SemaphoreType.DMA((3,)),
            pltpu.SemaphoreType.DMA((dp - 1,)),
            pltpu.SemaphoreType.DMA((dp - 1,)),
        ],
        compiler_params=pltpu.CompilerParams(
            collective_id=0, has_side_effects=True, vmem_limit_bytes=60 * 1024 * 1024
        ),
        name="triangle_updates",
    )(
        pair[0].reshape(channels, held).T,
        cotangent[0].reshape(channels, held).T,
        proj_weight,
        gate_weight,
        out_weight,
        proj_bias,
        chan_bias,
        norm_gain,
        norm_shift,
    )
    outputs = pl.pallas_call(
        deliver_kernel,
        out_shape=(
            jax.ShapeDtypeStruct((held, channels), jnp.bfloat16),
            jax.ShapeDtypeStruct((2, 4 * channels, channels), jnp.float32),
            jax.ShapeDtypeStruct((2, 4 * channels), jnp.float32),
            jax.ShapeDtypeStruct((2, channels, channels), jnp.float32),
            jax.ShapeDtypeStruct((2, channels, channels), jnp.float32),
            jax.ShapeDtypeStruct((2, 2, channels), jnp.float32),
            jax.ShapeDtypeStruct((2, 2, channels), jnp.float32),
            jax.ShapeDtypeStruct((2, 2, channels), jnp.float32),
        ),
        in_specs=[vmem] * 6,
        out_specs=(hbm,) * 8,
        scratch_shapes=[pltpu.SemaphoreType.DMA((8,))],
        name="deliver",
    )(*summed)
    return (outputs[0].T.reshape(1, channels, rows, width),) + tuple(outputs[1:])


def any_body(peers, pair, *others):
    _, channels, rows, width = pair.shape
    small = channels == 128 and width == 16 and rows % 4 == 0
    if small and peers[1] == 4 and peers[0] > 1:
        return fused_body(peers, pair, *others)
    return large_body(pair, *others)


def solution(mesh):
    in_specs = (
        P(("groups", "dp"), None, "dap", None),
        P(("groups", "dp"), None, "dap", None),
        P(),
        P(),
        P(),
        P(),
        P(),
        P(),
        P(),
    )
    out_specs = (
        P(("groups", "dp"), None, "dap", None),
        P("groups", None, None),
        P("groups", None),
        P("groups", None, None),
        P("groups", None, None),
        P("groups", None, None),
        P("groups", None, None),
        P("groups", None, None),
    )
    peers = (mesh.shape["dap"], mesh.shape["dp"])
    body = functools.partial(any_body, peers)
    return jax.shard_map(body, mesh=mesh, in_specs=in_specs, out_specs=out_specs, check_vma=False)
```

```python
import functools

import jax
import jax.numpy as jnp
from jax import lax
from jax.experimental import pallas as pl
from jax.experimental.pallas import tpu as pltpu
from jax.sharding import PartitionSpec as P

EPSILON = 1e-05


def normalize(values, scale_by, offset):
    average = jnp.mean(values, axis=0, keepdims=True)
    centred = values - average
    variance = jnp.mean(centred * centred, axis=0, keepdims=True)
    inverse = lax.rsqrt(variance + EPSILON)
    standard = centred * inverse
    return (standard * scale_by[:, None] + offset[:, None], standard, inverse)


def normalize_back(upstream, scale_by, standard, inverse):
    scaled = upstream * scale_by[:, None]
    adjusted = (
        scaled
        - jnp.mean(scaled, axis=0, keepdims=True)
        - standard * jnp.mean(scaled * standard, axis=0, keepdims=True)
    )
    return (inverse * adjusted, jnp.sum(upstream * standard, axis=1), jnp.sum(upstream, axis=1))


def matmul_rows(left, right):
    return lax.dot_general(
        left, right, (((1,), (1,)), ((), ())), preferred_element_type=jnp.float32
    )


def matmul_cols(left, right):
    return lax.dot_general(
        left, right, (((0,), (0,)), ((), ())), preferred_element_type=jnp.float32
    )


def contract(left, right, left_dim, right_dim):
    return lax.dot_general(
        left, right, (((left_dim,), (right_dim,)), ((0,), (0,))), preferred_element_type=jnp.float32
    )


def forward_update(pair_rows, params, layer, dims, incoming):
    proj_weight, proj_bias, gate_weight, out_weight, chan_bias, norm_gain, norm_shift = params
    channels, rows, width = dims
    source = pair_rows.astype(jnp.float32)
    normed, standard_in, inverse_in = normalize(source, norm_gain[layer, 0], norm_shift[layer, 0])
    inputs = normed.astype(jnp.bfloat16)
    weight_now = proj_weight[layer]
    bias_now = proj_bias[layer]

    def gated(first_row):
        pre_act = jnp.dot(
            weight_now[first_row : first_row + 2 * channels],
            inputs,
            preferred_element_type=jnp.float32,
        )
        pre_act = pre_act + bias_now[first_row : first_row + 2 * channels][:, None]
        value = pre_act[:channels]
        logit = pre_act[channels:]
        product = (
            (jax.nn.sigmoid(logit) * value).astype(jnp.bfloat16).reshape(channels, rows, width)
        )
        return (product, value, logit)

    left_rows, left_value, left_logit = gated(0)
    left_cols = lax.all_to_all(left_rows, "dap", split_axis=0, concat_axis=1, tiled=True)
    right_rows, right_value, right_logit = gated(2 * channels)
    right_cols = lax.all_to_all(right_rows, "dap", split_axis=0, concat_axis=1, tiled=True)
    gate = jax.nn.sigmoid(
        jnp.dot(gate_weight[layer], inputs, preferred_element_type=jnp.float32)
        + chan_bias[layer, 0][:, None]
    )
    if incoming:
        triangle = contract(left_cols, right_cols, 1, 1)
    else:
        triangle = contract(left_cols, right_cols, 2, 2)
    triangle_rows = lax.all_to_all(
        triangle.astype(jnp.bfloat16), "dap", split_axis=1, concat_axis=0, tiled=True
    )
    triangle_rows = triangle_rows.reshape(channels, rows * width)
    normed_tri, standard_out, inverse_out = normalize(
        triangle_rows.astype(jnp.float32), norm_gain[layer, 1], norm_shift[layer, 1]
    )
    tri_inputs = normed_tri.astype(jnp.bfloat16)
    linear = (
        jnp.dot(out_weight[layer], tri_inputs, preferred_element_type=jnp.float32)
        + chan_bias[layer, 1][:, None]
    )
    next_pair = (source + gate * linear).astype(jnp.bfloat16)
    saved = (
        inputs,
        standard_in,
        inverse_in,
        left_value,
        left_logit,
        right_value,
        right_logit,
        left_cols,
        right_cols,
        gate,
        linear,
        tri_inputs,
        standard_out,
        inverse_out,
    )
    return (next_pair, saved)


def backward_update(upstream, saved, params, layer, dims, incoming):
    proj_weight, proj_bias, gate_weight, out_weight, chan_bias, norm_gain, norm_shift = params
    channels, rows, width = dims
    (
        inputs,
        standard_in,
        inverse_in,
        left_value,
        left_logit,
        right_value,
        right_logit,
        left_cols,
        right_cols,
        gate,
        linear,
        tri_inputs,
        standard_out,
        inverse_out,
    ) = saved
    grad_linear = (upstream * gate).astype(jnp.bfloat16)
    grad_logit = (upstream * linear * gate * (1.0 - gate)).astype(jnp.bfloat16)
    grad_out_w = matmul_rows(grad_linear, tri_inputs)
    grad_out_b = jnp.sum(grad_linear.astype(jnp.float32), axis=1)
    grad_gate_w = matmul_rows(grad_logit, inputs)
    grad_gate_b = jnp.sum(grad_logit.astype(jnp.float32), axis=1)
    grad_normed = matmul_cols(out_weight[layer], grad_linear)
    grad_tri, gain_out, shift_out = normalize_back(
        grad_normed, norm_gain[layer, 1], standard_out, inverse_out
    )
    grad_cols = lax.all_to_all(
        grad_tri.astype(jnp.bfloat16).reshape(channels, rows, width),
        "dap",
        split_axis=0,
        concat_axis=1,
        tiled=True,
    )

    def left_term():
        if incoming:
            return contract(right_cols, grad_cols, 2, 2).astype(jnp.bfloat16)
        return contract(grad_cols, right_cols, 2, 1).astype(jnp.bfloat16)

    def right_term():
        if incoming:
            return contract(left_cols, grad_cols, 2, 1).astype(jnp.bfloat16)
        return contract(grad_cols, left_cols, 1, 1).astype(jnp.bfloat16)

    left_back = lax.all_to_all(left_term(), "dap", split_axis=1, concat_axis=0, tiled=True)
    right_back = lax.all_to_all(right_term(), "dap", split_axis=1, concat_axis=0, tiled=True)
    left_back = left_back.reshape(channels, rows * width).astype(jnp.float32)
    right_back = right_back.reshape(channels, rows * width).astype(jnp.float32)
    left_sig = jax.nn.sigmoid(left_logit)
    right_sig = jax.nn.sigmoid(right_logit)
    grad_pre = jnp.concatenate(
        [
            left_back * left_sig,
            left_back * left_value * left_sig * (1.0 - left_sig),
            right_back * right_sig,
            right_back * right_value * right_sig * (1.0 - right_sig),
        ],
        axis=0,
    ).astype(jnp.bfloat16)
    grad_proj_w = matmul_rows(grad_pre, inputs)
    grad_proj_b = jnp.sum(grad_pre.astype(jnp.float32), axis=1)
    grad_inputs = matmul_cols(proj_weight[layer], grad_pre) + matmul_cols(
        gate_weight[layer], grad_logit
    )
    grad_source, gain_in, shift_in = normalize_back(
        grad_inputs, norm_gain[layer, 0], standard_in, inverse_in
    )
    grads = (
        grad_proj_w,
        grad_proj_b,
        grad_gate_w,
        grad_out_w,
        jnp.stack([grad_gate_b, grad_out_b]),
        jnp.stack([gain_in, gain_out]),
        jnp.stack([shift_in, shift_out]),
    )
    return (upstream + grad_source, grads)


def large_body(
    pair,
    cotangent,
    proj_weight,
    proj_bias,
    gate_weight,
    out_weight,
    chan_bias,
    norm_gain,
    norm_shift,
):
    params = (proj_weight, proj_bias, gate_weight, out_weight, chan_bias, norm_gain, norm_shift)
    channels = pair.shape[1]
    rows = pair.shape[2]
    width = pair.shape[3]
    dims = (channels, rows, width)
    start_pair = pair[0].reshape(channels, rows * width)
    middle, saved_first = forward_update(start_pair, params, 0, dims, False)
    unused, saved_second = forward_update(middle, params, 1, dims, True)
    upstream = cotangent[0].reshape(channels, rows * width).astype(jnp.float32)
    grad_middle, grads_second = backward_update(upstream, saved_second, params, 1, dims, True)
    repeat_pair, saved_first = forward_update(start_pair, params, 0, dims, False)
    grad_start, grads_first = backward_update(grad_middle, saved_first, params, 0, dims, False)
    joined = tuple(
        (
            jnp.stack([first_part, second_part])
            for first_part, second_part in zip(grads_first, grads_second)
        )
    )
    stacked = lax.psum(
        (joined[0], joined[1], joined[2], joined[3], joined[4], joined[5], joined[6]), ("dap", "dp")
    )
    factor = 1.0 / width
    return (
        grad_start.astype(jnp.bfloat16).reshape(1, channels, rows, width),
        stacked[0] * factor,
        stacked[1] * factor,
        stacked[2] * factor,
        stacked[3] * factor,
        stacked[4] * factor,
        stacked[5] * factor,
        stacked[6] * factor,
    )


def norm_lanes(values, scale_by, offset):
    average = jnp.mean(values, axis=1, keepdims=True)
    centred = values - average
    variance = jnp.mean(centred * centred, axis=1, keepdims=True)
    inverse = lax.rsqrt(variance + EPSILON)
    standard = centred * inverse
    return (standard * scale_by + offset, standard, inverse)


def norm_lanes_back(upstream, scale_by, standard, inverse):
    scaled = upstream * scale_by
    adjusted = (
        scaled
        - jnp.mean(scaled, axis=1, keepdims=True)
        - standard * jnp.mean(scaled * standard, axis=1, keepdims=True)
    )
    return inverse * adjusted


def column_sum(values):
    return jnp.sum(values, axis=0, keepdims=True)


def rounded(values):
    return values.astype(jnp.bfloat16).astype(jnp.float32)


def products(width, a_ref, a_turned, b_ref, b_turned, o_ref):
    blocks = [
        b_ref[pl.ds(m, width, stride=width), :] if b_turned else b_ref[pl.ds(m * width, width), :]
        for m in range(width)
    ]

    def step(p, carry):
        total = None
        for m in range(width):
            row = a_ref[pl.ds(m * width + p if a_turned else p * width + m, 1), :]
            term = row * blocks[m]
            total = term if total is None else total + term
        o_ref[pl.ds(p * width, width), :] = total
        return carry

    for p in range(width):
        step(p, 0)


def fused_kernel(
    peers,
    width,
    pair_hbm,
    cot_hbm,
    proj_hbm,
    gate_hbm,
    outw_hbm,
    bias_hbm,
    chan_hbm,
    gain_hbm,
    shift_hbm,
    dpair_ref,
    big_ref,
    dbias_ref,
    dchan_ref,
    dgain_ref,
    dshift_ref,
    proj_ref,
    gate_ref,
    outw_ref,
    bias_ref,
    chan_ref,
    gain_ref,
    shift_ref,
    pair_all,
    cot_all,
    left_s,
    right_s,
    tri_s,
    grad_s,
    dleft_s,
    dright_s,
    rows_s,
    send_half,
    recv_half,
    send_sum,
    recv_sum,
    small_all,
    fetch_done,
    gather_send,
    gather_recv,
    half_send,
    half_recv,
    sum_send,
    sum_recv,
    share_send,
    share_recv,
    small_send,
    small_recv,
):
    dap, dp = peers
    mesh_ids = pl.DeviceIdType.MESH
    held, channels = pair_hbm.shape
    me = lax.axis_index("dap")
    at = lax.axis_index("dp")
    core = lax.rem(at, 2)
    core_peer = at + 1 - 2 * core
    far_peer = lax.rem(at + 2, dp)

    own = pl.ds(pl.multiple_of(me * held, held), held)
    fetches = []
    for source, target in (
        (pair_hbm, pair_all.at[own]),
        (cot_hbm, cot_all.at[own]),
        (gain_hbm, gain_ref),
        (shift_hbm, shift_ref),
        (proj_hbm, proj_ref),
        (bias_hbm, bias_ref),
        (gate_hbm, gate_ref),
        (chan_hbm, chan_ref),
        (outw_hbm, outw_ref),
    ):
        copy = pltpu.make_async_copy(source, target, fetch_done.at[len(fetches)])
        copy.start()
        fetches.append(copy)

    barrier = pltpu.get_barrier_semaphore()
    for k in range(1, dap):
        pl.semaphore_signal(
            barrier, inc=1, device_id={"dap": lax.rem(me + k, dap)}, device_id_type=mesh_ids
        )
    for k in range(1, dp):
        pl.semaphore_signal(
            barrier, inc=1, device_id={"dp": lax.rem(at + k, dp)}, device_id_type=mesh_ids
        )
    pl.semaphore_wait(barrier, dap + dp - 2)

    gathers = []
    for slot, whole in enumerate((pair_all, cot_all)):
        fetches[slot].wait()
        copies = []
        for k in range(1, dap):
            copy = pltpu.make_async_remote_copy(
                src_ref=whole.at[own],
                dst_ref=whole.at[own],
                send_sem=gather_send.at[slot, k - 1],
                recv_sem=gather_recv.at[slot, k - 1],
                device_id={"dap": lax.rem(me + k, dap)},
                device_id_type=mesh_ids,
            )
            copy.start()
            copies.append(copy)
        gathers.append(copies)

    factor = 1.0 / width

    def forward(source, layer):
        normed, standard_in, inverse_in = norm_lanes(
            source, gain_ref[layer, 0:1, :], shift_ref[layer, 0:1, :]
        )
        inputs = normed.astype(jnp.bfloat16)
        pre_act = matmul_rows(inputs, proj_ref[layer]) + bias_ref[layer : layer + 1, :]
        left_value = pre_act[:, :channels]
        left_sig = jax.nn.sigmoid(pre_act[:, channels : 2 * channels])
        right_value = pre_act[:, 2 * channels : 3 * channels]
        right_sig = jax.nn.sigmoid(pre_act[:, 3 * channels :])
        left_s[layer] = rounded(left_sig * left_value)
        right_s[layer] = rounded(right_sig * right_value)
        gate = jax.nn.sigmoid(matmul_rows(inputs, gate_ref[layer]) + chan_ref[layer, 0:1, :])
        left, right = left_s.at[layer], right_s.at[layer]
        if layer == 0:
            products(width, left, False, right, True, tri_s)
        else:
            products(width, left, True, right, False, tri_s)
        normed_tri, standard_out, inverse_out = norm_lanes(
            rounded(tri_s[...]), gain_ref[layer, 1:2, :], shift_ref[layer, 1:2, :]
        )
        tri_inputs = normed_tri.astype(jnp.bfloat16)
        linear = matmul_rows(tri_inputs, outw_ref[layer]) + chan_ref[layer, 1:2, :]
        saved = (
            inputs,
            standard_in,
            inverse_in,
            left_value,
            left_sig,
            right_value,
            right_sig,
            gate,
            linear,
            tri_inputs,
            standard_out,
            inverse_out,
        )
        return saved

    def put_small(layer, row, values):
        rows_s[layer, row : row + 1, :] = values * factor

    def backward_near(upstream, saved, layer):
        inputs, _, _, _, _, _, _, gate, linear, tri_inputs, standard_out, inverse_out = saved
        grad_linear = (upstream * gate).astype(jnp.bfloat16)
        grad_logit = (upstream * linear * gate * (1.0 - gate)).astype(jnp.bfloat16)
        grad_normed = jnp.dot(grad_linear, outw_ref[layer], preferred_element_type=jnp.float32)
        grad_s[...] = rounded(
            norm_lanes_back(grad_normed, gain_ref[layer, 1:2, :], standard_out, inverse_out)
        )
        big_ref[layer, 4 * channels : 5 * channels, :] = matmul_cols(grad_logit, inputs) * factor
        big_ref[layer, 5 * channels :, :] = matmul_cols(grad_linear, tri_inputs) * factor
        put_small(layer, 4, column_sum(grad_logit.astype(jnp.float32)))
        put_small(layer, 5, column_sum(grad_linear.astype(jnp.float32)))
        put_small(layer, 7, column_sum(grad_normed * standard_out))
        put_small(layer, 9, column_sum(grad_normed))
        return grad_logit

    def backward_far(upstream, saved, grad_logit, layer):
        inputs, standard_in, inverse_in, left_value, left_sig, right_value, right_sig = saved[:7]
        left, right = left_s.at[layer], right_s.at[layer]
        if layer == 0:
            products(width, grad_s, False, right, False, dleft_s)
            products(width, grad_s, True, left, False, dright_s)
        else:
            products(width, right, False, grad_s, True, dleft_s)
            products(width, left, False, grad_s, False, dright_s)
        left_back = rounded(dleft_s[...])
        right_back = rounded(dright_s[...])
        blocks = (
            left_back * left_sig,
            left_back * left_value * left_sig * (1.0 - left_sig),
            right_back * right_sig,
            right_back * right_value * right_sig * (1.0 - right_sig),
        )
        grad_inputs = jnp.dot(grad_logit, gate_ref[layer], preferred_element_type=jnp.float32)
        for index, block in enumerate(blocks):
            part = block.astype(jnp.bfloat16)
            lines = slice(index * channels, (index + 1) * channels)
            big_ref[layer, lines, :] = matmul_cols(part, inputs) * factor
            put_small(layer, index, column_sum(part.astype(jnp.float32)))
            grad_inputs = grad_inputs + jnp.dot(
                part, proj_ref[layer, lines, :], preferred_element_type=jnp.float32
            )
            if index % 2 == 1 and layer == 0:
                exchange_half(2 + index // 2)
        put_small(layer, 6, column_sum(grad_inputs * standard_in))
        put_small(layer, 8, column_sum(grad_inputs))
        return upstream + norm_lanes_back(
            grad_inputs, gain_ref[layer, 0:1, :], standard_in, inverse_in
        )

    pieces = (
        (1, 0, 6 * channels),
        (0, 4 * channels, 2 * channels),
        (0, 0, 2 * channels),
        (0, 2 * channels, 2 * channels),
    )
    flights = {}

    def spans(index):
        layer, first, count = pieces[index]
        half = count // 2
        mine = pl.ds(pl.multiple_of(first + core * half, half), half)
        other = pl.ds(pl.multiple_of(first + (1 - core) * half, half), half)
        slot = pl.ds(sum(piece[2] // 2 for piece in pieces[:index]), half)
        return (big_ref.at[layer], mine, other, slot)

    def exchange_half(index):
        whole, mine, other, slot = spans(index)
        send_half[slot, :] = whole[other, :].astype(jnp.bfloat16)
        copy = pltpu.make_async_remote_copy(
            src_ref=send_half.at[slot],
            dst_ref=recv_half.at[slot],
            send_sem=half_send.at[index],
            recv_sem=half_recv.at[index],
            device_id={"dp": core_peer},
            device_id_type=mesh_ids,
        )
        copy.start()
        flights[index] = [copy]

    def exchange_sum(index):
        whole, mine, other, slot = spans(index)
        flights[index][0].wait_recv()
        added = whole[mine, :] + recv_half[slot, :].astype(jnp.float32)
        send_sum[slot, :] = added.astype(jnp.bfloat16)
        copy = pltpu.make_async_remote_copy(
            src_ref=send_sum.at[slot],
            dst_ref=recv_sum.at[slot],
            send_sem=sum_send.at[index],
            recv_sem=sum_recv.at[index],
            device_id={"dp": far_peer},
            device_id_type=mesh_ids,
        )
        copy.start()
        flights[index].append(copy)

    def share(index):
        whole, mine, other, slot = spans(index)
        flights[index][1].wait_recv()
        whole[mine, :] = send_sum[slot, :].astype(jnp.float32) + recv_sum[slot, :].astype(
            jnp.float32
        )
        copy = pltpu.make_async_remote_copy(
            src_ref=whole.at[mine],
            dst_ref=whole.at[mine],
            send_sem=share_send.at[index],
            recv_sem=share_recv.at[index],
            device_id={"dp": core_peer},
            device_id_type=mesh_ids,
        )
        copy.start()
        flights[index].append(copy)

    for copy in fetches[2:]:
        copy.wait()
    for copy in gathers[0]:
        copy.wait_recv()
    start_pair = pair_all[...].astype(jnp.float32)
    saved_first = forward(start_pair, 0)
    middle = rounded(start_pair + saved_first[7] * saved_first[8])
    saved_second = forward(middle, 1)
    for copy in gathers[1]:
        copy.wait_recv()
    upstream = cot_all[...].astype(jnp.float32)
    grad_logit = backward_near(upstream, saved_second, 1)
    grad_middle = backward_far(upstream, saved_second, grad_logit, 1)
    exchange_half(0)
    grad_logit = backward_near(grad_middle, saved_first, 0)
    exchange_half(1)
    exchange_sum(0)
    exchange_sum(1)
    grad_start = backward_far(grad_middle, saved_first, grad_logit, 0)
    small_all[at] = rows_s[...]
    small_copies = []
    for k in range(1, dp):
        copy = pltpu.make_async_remote_copy(
            src_ref=rows_s,
            dst_ref=small_all.at[at],
            send_sem=small_send.at[k - 1],
            recv_sem=small_recv.at[k - 1],
            device_id={"dp": lax.rem(at + k, dp)},
            device_id_type=mesh_ids,
        )
        copy.start()
        small_copies.append(copy)
    exchange_sum(2)
    exchange_sum(3)
    dleft_s[...] = grad_start
    dpair_ref[...] = dleft_s[own, :].astype(jnp.bfloat16)
    share(0)
    share(1)
    for copy in small_copies:
        copy.wait_recv()
    total = small_all[0]
    for index in range(1, dp):
        total = total + small_all[index]
    for index in range(4):
        dbias_ref[:, index * channels : (index + 1) * channels] = total[:, index]
    dchan_ref[...] = total[:, 4:6]
    dgain_ref[...] = total[:, 6:8]
    dshift_ref[...] = total[:, 8:10]
    share(2)
    share(3)
    for index in range(4):
        flights[index][2].wait_recv()
    for index in range(4):
        for copy in flights[index]:
            copy.wait_send()
    for copy in gathers[0] + gathers[1] + small_copies:
        copy.wait_send()


def deliver_kernel(
    dpair_ref,
    big_ref,
    dbias_ref,
    dchan_ref,
    dgain_ref,
    dshift_ref,
    dpair_out,
    proj_out,
    bias_out,
    gate_out,
    outw_out,
    chan_out,
    gain_out,
    shift_out,
    done,
):
    channels = big_ref.shape[2]
    copies = []
    for source, target in (
        (big_ref.at[:, : 4 * channels], proj_out),
        (big_ref.at[:, 4 * channels : 5 * channels], gate_out),
        (big_ref.at[:, 5 * channels :], outw_out),
        (dpair_ref, dpair_out),
        (dbias_ref, bias_out),
        (dchan_ref, chan_out),
        (dgain_ref, gain_out),
        (dshift_ref, shift_out),
    ):
        copy = pltpu.make_async_copy(source, target, done.at[len(copies)])
        copy.start()
        copies.append(copy)
    for copy in copies:
        copy.wait()


def fused_body(
    peers,
    pair,
    cotangent,
    proj_weight,
    proj_bias,
    gate_weight,
    out_weight,
    chan_bias,
    norm_gain,
    norm_shift,
):
    dap, dp = peers
    _, channels, rows, width = pair.shape
    held = rows * width
    entries = width * width
    float_rows = pltpu.VMEM((entries, channels), jnp.float32)
    layer_rows = pltpu.VMEM((2, entries, channels), jnp.float32)
    half_rows = pltpu.VMEM((6 * channels, channels), jnp.bfloat16)
    vmem = pl.BlockSpec(memory_space=pltpu.VMEM)
    hbm = pl.BlockSpec(memory_space=pltpu.HBM)
    summed = pl.pallas_call(
        functools.partial(fused_kernel, peers, width),
        out_shape=(
            pltpu.VMEM((held, channels), jnp.bfloat16),
            pltpu.VMEM((2, 6 * channels, channels), jnp.float32),
            pltpu.VMEM((2, 4 * channels), jnp.float32),
            pltpu.VMEM((2, 2, channels), jnp.float32),
            pltpu.VMEM((2, 2, channels), jnp.float32),
            pltpu.VMEM((2, 2, channels), jnp.float32),
        ),
        in_specs=[hbm] * 9,
        out_specs=(vmem,) * 6,
        scratch_shapes=[
            pltpu.VMEM(proj_weight.shape, jnp.bfloat16),
            pltpu.VMEM(gate_weight.shape, jnp.bfloat16),
            pltpu.VMEM(out_weight.shape, jnp.bfloat16),
            pltpu.VMEM(proj_bias.shape, jnp.float32),
            pltpu.VMEM(chan_bias.shape, jnp.float32),
            pltpu.VMEM(norm_gain.shape, jnp.float32),
            pltpu.VMEM(norm_shift.shape, jnp.float32),
            pltpu.VMEM((entries, channels), jnp.bfloat16),
            pltpu.VMEM((entries, channels), jnp.bfloat16),
            layer_rows,
            layer_rows,
            float_rows,
            float_rows,
            float_rows,
            float_rows,
            pltpu.VMEM((2, 10, channels), jnp.float32),
            half_rows,
            half_rows,
            half_rows,
            half_rows,
            pltpu.VMEM((dp, 2, 10, channels), jnp.float32),
            pltpu.SemaphoreType.DMA((9,)),
            pltpu.SemaphoreType.DMA((2, dap - 1)),
            pltpu.SemaphoreType.DMA((2, dap - 1)),
            pltpu.SemaphoreType.DMA((4,)),
            pltpu.SemaphoreType.DMA((4,)),
            pltpu.SemaphoreType.DMA((4,)),
            pltpu.SemaphoreType.DMA((4,)),
            pltpu.SemaphoreType.DMA((4,)),
            pltpu.SemaphoreType.DMA((4,)),
            pltpu.SemaphoreType.DMA((dp - 1,)),
            pltpu.SemaphoreType.DMA((dp - 1,)),
        ],
        compiler_params=pltpu.CompilerParams(
            collective_id=0, has_side_effects=True, vmem_limit_bytes=60 * 1024 * 1024
        ),
        name="triangle_updates",
    )(
        pair[0].reshape(channels, held).T,
        cotangent[0].reshape(channels, held).T,
        proj_weight,
        gate_weight,
        out_weight,
        proj_bias,
        chan_bias,
        norm_gain,
        norm_shift,
    )
    outputs = pl.pallas_call(
        deliver_kernel,
        out_shape=(
            jax.ShapeDtypeStruct((held, channels), jnp.bfloat16),
            jax.ShapeDtypeStruct((2, 4 * channels, channels), jnp.float32),
            jax.ShapeDtypeStruct((2, 4 * channels), jnp.float32),
            jax.ShapeDtypeStruct((2, channels, channels), jnp.float32),
            jax.ShapeDtypeStruct((2, channels, channels), jnp.float32),
            jax.ShapeDtypeStruct((2, 2, channels), jnp.float32),
            jax.ShapeDtypeStruct((2, 2, channels), jnp.float32),
            jax.ShapeDtypeStruct((2, 2, channels), jnp.float32),
        ),
        in_specs=[vmem] * 6,
        out_specs=(hbm,) * 8,
        scratch_shapes=[pltpu.SemaphoreType.DMA((8,))],
        compiler_params=pltpu.CompilerParams(vmem_limit_bytes=4 * 1024 * 1024),
        name="deliver",
    )(*summed)
    return (outputs[0].T.reshape(1, channels, rows, width),) + tuple(outputs[1:])


def any_body(peers, pair, *others):
    _, channels, rows, width = pair.shape
    small = channels == 128 and width == 16 and rows % 4 == 0
    if small and peers[1] == 4 and peers[0] > 1:
        return fused_body(peers, pair, *others)
    return large_body(pair, *others)


def solution(mesh):
    in_specs = (
        P(("groups", "dp"), None, "dap", None),
        P(("groups", "dp"), None, "dap", None),
        P(),
        P(),
        P(),
        P(),
        P(),
        P(),
        P(),
    )
    out_specs = (
        P(("groups", "dp"), None, "dap", None),
        P("groups", None, None),
        P("groups", None),
        P("groups", None, None),
        P("groups", None, None),
        P("groups", None, None),
        P("groups", None, None),
        P("groups", None, None),
    )
    peers = (mesh.shape["dap"], mesh.shape["dp"])
    body = functools.partial(any_body, peers)
    return jax.shard_map(body, mesh=mesh, in_specs=in_specs, out_specs=out_specs, check_vma=False)
```

```python
import functools

import jax
import jax.numpy as jnp
from jax import lax
from jax.experimental import pallas as pl
from jax.experimental.pallas import tpu as pltpu
from jax.sharding import PartitionSpec as P

EPSILON = 1e-05


def normalize(values, scale_by, offset):
    average = jnp.mean(values, axis=0, keepdims=True)
    centred = values - average
    variance = jnp.mean(centred * centred, axis=0, keepdims=True)
    inverse = lax.rsqrt(variance + EPSILON)
    standard = centred * inverse
    return (standard * scale_by[:, None] + offset[:, None], standard, inverse)


def normalize_back(upstream, scale_by, standard, inverse):
    scaled = upstream * scale_by[:, None]
    adjusted = (
        scaled
        - jnp.mean(scaled, axis=0, keepdims=True)
        - standard * jnp.mean(scaled * standard, axis=0, keepdims=True)
    )
    return (inverse * adjusted, jnp.sum(upstream * standard, axis=1), jnp.sum(upstream, axis=1))


def matmul_rows(left, right):
    return lax.dot_general(
        left, right, (((1,), (1,)), ((), ())), preferred_element_type=jnp.float32
    )


def matmul_cols(left, right):
    return lax.dot_general(
        left, right, (((0,), (0,)), ((), ())), preferred_element_type=jnp.float32
    )


def contract(left, right, left_dim, right_dim):
    return lax.dot_general(
        left, right, (((left_dim,), (right_dim,)), ((0,), (0,))), preferred_element_type=jnp.float32
    )


def forward_update(pair_rows, params, layer, dims, incoming):
    proj_weight, proj_bias, gate_weight, out_weight, chan_bias, norm_gain, norm_shift = params
    channels, rows, width = dims
    source = pair_rows.astype(jnp.float32)
    normed, standard_in, inverse_in = normalize(source, norm_gain[layer, 0], norm_shift[layer, 0])
    inputs = normed.astype(jnp.bfloat16)
    weight_now = proj_weight[layer]
    bias_now = proj_bias[layer]

    def gated(first_row):
        pre_act = jnp.dot(
            weight_now[first_row : first_row + 2 * channels],
            inputs,
            preferred_element_type=jnp.float32,
        )
        pre_act = pre_act + bias_now[first_row : first_row + 2 * channels][:, None]
        value = pre_act[:channels]
        logit = pre_act[channels:]
        product = (
            (jax.nn.sigmoid(logit) * value).astype(jnp.bfloat16).reshape(channels, rows, width)
        )
        return (product, value, logit)

    left_rows, left_value, left_logit = gated(0)
    left_cols = lax.all_to_all(left_rows, "dap", split_axis=0, concat_axis=1, tiled=True)
    right_rows, right_value, right_logit = gated(2 * channels)
    right_cols = lax.all_to_all(right_rows, "dap", split_axis=0, concat_axis=1, tiled=True)
    gate = jax.nn.sigmoid(
        jnp.dot(gate_weight[layer], inputs, preferred_element_type=jnp.float32)
        + chan_bias[layer, 0][:, None]
    )
    if incoming:
        triangle = contract(left_cols, right_cols, 1, 1)
    else:
        triangle = contract(left_cols, right_cols, 2, 2)
    triangle_rows = lax.all_to_all(
        triangle.astype(jnp.bfloat16), "dap", split_axis=1, concat_axis=0, tiled=True
    )
    triangle_rows = triangle_rows.reshape(channels, rows * width)
    normed_tri, standard_out, inverse_out = normalize(
        triangle_rows.astype(jnp.float32), norm_gain[layer, 1], norm_shift[layer, 1]
    )
    tri_inputs = normed_tri.astype(jnp.bfloat16)
    linear = (
        jnp.dot(out_weight[layer], tri_inputs, preferred_element_type=jnp.float32)
        + chan_bias[layer, 1][:, None]
    )
    next_pair = (source + gate * linear).astype(jnp.bfloat16)
    saved = (
        inputs,
        standard_in,
        inverse_in,
        left_value,
        left_logit,
        right_value,
        right_logit,
        left_cols,
        right_cols,
        gate,
        linear,
        tri_inputs,
        standard_out,
        inverse_out,
    )
    return (next_pair, saved)


def backward_update(upstream, saved, params, layer, dims, incoming):
    proj_weight, proj_bias, gate_weight, out_weight, chan_bias, norm_gain, norm_shift = params
    channels, rows, width = dims
    (
        inputs,
        standard_in,
        inverse_in,
        left_value,
        left_logit,
        right_value,
        right_logit,
        left_cols,
        right_cols,
        gate,
        linear,
        tri_inputs,
        standard_out,
        inverse_out,
    ) = saved
    grad_linear = (upstream * gate).astype(jnp.bfloat16)
    grad_logit = (upstream * linear * gate * (1.0 - gate)).astype(jnp.bfloat16)
    grad_out_w = matmul_rows(grad_linear, tri_inputs)
    grad_out_b = jnp.sum(grad_linear.astype(jnp.float32), axis=1)
    grad_gate_w = matmul_rows(grad_logit, inputs)
    grad_gate_b = jnp.sum(grad_logit.astype(jnp.float32), axis=1)
    grad_normed = matmul_cols(out_weight[layer], grad_linear)
    grad_tri, gain_out, shift_out = normalize_back(
        grad_normed, norm_gain[layer, 1], standard_out, inverse_out
    )
    grad_cols = lax.all_to_all(
        grad_tri.astype(jnp.bfloat16).reshape(channels, rows, width),
        "dap",
        split_axis=0,
        concat_axis=1,
        tiled=True,
    )

    def left_term():
        if incoming:
            return contract(right_cols, grad_cols, 2, 2).astype(jnp.bfloat16)
        return contract(grad_cols, right_cols, 2, 1).astype(jnp.bfloat16)

    def right_term():
        if incoming:
            return contract(left_cols, grad_cols, 2, 1).astype(jnp.bfloat16)
        return contract(grad_cols, left_cols, 1, 1).astype(jnp.bfloat16)

    left_back = lax.all_to_all(left_term(), "dap", split_axis=1, concat_axis=0, tiled=True)
    right_back = lax.all_to_all(right_term(), "dap", split_axis=1, concat_axis=0, tiled=True)
    left_back = left_back.reshape(channels, rows * width).astype(jnp.float32)
    right_back = right_back.reshape(channels, rows * width).astype(jnp.float32)
    left_sig = jax.nn.sigmoid(left_logit)
    right_sig = jax.nn.sigmoid(right_logit)
    grad_pre = jnp.concatenate(
        [
            left_back * left_sig,
            left_back * left_value * left_sig * (1.0 - left_sig),
            right_back * right_sig,
            right_back * right_value * right_sig * (1.0 - right_sig),
        ],
        axis=0,
    ).astype(jnp.bfloat16)
    grad_proj_w = matmul_rows(grad_pre, inputs)
    grad_proj_b = jnp.sum(grad_pre.astype(jnp.float32), axis=1)
    grad_inputs = matmul_cols(proj_weight[layer], grad_pre) + matmul_cols(
        gate_weight[layer], grad_logit
    )
    grad_source, gain_in, shift_in = normalize_back(
        grad_inputs, norm_gain[layer, 0], standard_in, inverse_in
    )
    grads = (
        grad_proj_w,
        grad_proj_b,
        grad_gate_w,
        grad_out_w,
        jnp.stack([grad_gate_b, grad_out_b]),
        jnp.stack([gain_in, gain_out]),
        jnp.stack([shift_in, shift_out]),
    )
    return (upstream + grad_source, grads)


def large_body(
    pair,
    cotangent,
    proj_weight,
    proj_bias,
    gate_weight,
    out_weight,
    chan_bias,
    norm_gain,
    norm_shift,
):
    params = (proj_weight, proj_bias, gate_weight, out_weight, chan_bias, norm_gain, norm_shift)
    channels = pair.shape[1]
    rows = pair.shape[2]
    width = pair.shape[3]
    dims = (channels, rows, width)
    start_pair = pair[0].reshape(channels, rows * width)
    middle, saved_first = forward_update(start_pair, params, 0, dims, False)
    unused, saved_second = forward_update(middle, params, 1, dims, True)
    upstream = cotangent[0].reshape(channels, rows * width).astype(jnp.float32)
    grad_middle, grads_second = backward_update(upstream, saved_second, params, 1, dims, True)
    repeat_pair, saved_first = forward_update(start_pair, params, 0, dims, False)
    grad_start, grads_first = backward_update(grad_middle, saved_first, params, 0, dims, False)
    joined = tuple(
        (
            jnp.stack([first_part, second_part])
            for first_part, second_part in zip(grads_first, grads_second)
        )
    )
    stacked = lax.psum(
        (joined[0], joined[1], joined[2], joined[3], joined[4], joined[5], joined[6]), ("dap", "dp")
    )
    factor = 1.0 / width
    return (
        grad_start.astype(jnp.bfloat16).reshape(1, channels, rows, width),
        stacked[0] * factor,
        stacked[1] * factor,
        stacked[2] * factor,
        stacked[3] * factor,
        stacked[4] * factor,
        stacked[5] * factor,
        stacked[6] * factor,
    )


def norm_lanes(values, scale_by, offset):
    average = jnp.mean(values, axis=1, keepdims=True)
    centred = values - average
    variance = jnp.mean(centred * centred, axis=1, keepdims=True)
    inverse = lax.rsqrt(variance + EPSILON)
    standard = centred * inverse
    return (standard * scale_by + offset, standard, inverse)


def norm_lanes_back(upstream, scale_by, standard, inverse):
    scaled = upstream * scale_by
    adjusted = (
        scaled
        - jnp.mean(scaled, axis=1, keepdims=True)
        - standard * jnp.mean(scaled * standard, axis=1, keepdims=True)
    )
    return inverse * adjusted


def column_sum(values):
    return jnp.sum(values, axis=0, keepdims=True)


def rounded(values):
    return values.astype(jnp.bfloat16).astype(jnp.float32)


def products(width, a_ref, a_turned, b_ref, b_turned, o_ref):
    blocks = [
        b_ref[pl.ds(m, width, stride=width), :] if b_turned else b_ref[pl.ds(m * width, width), :]
        for m in range(width)
    ]

    def step(p, carry):
        total = None
        for m in range(width):
            row = a_ref[pl.ds(m * width + p if a_turned else p * width + m, 1), :]
            term = row * blocks[m]
            total = term if total is None else total + term
        o_ref[pl.ds(p * width, width), :] = total
        return carry

    for p in range(width):
        step(p, 0)


def fused_kernel(
    peers,
    width,
    pair_hbm,
    cot_hbm,
    proj_hbm,
    gate_hbm,
    outw_hbm,
    bias_hbm,
    chan_hbm,
    gain_hbm,
    shift_hbm,
    dpair_ref,
    big_ref,
    dbias_ref,
    dchan_ref,
    dgain_ref,
    dshift_ref,
    proj_ref,
    gate_ref,
    outw_ref,
    bias_ref,
    chan_ref,
    gain_ref,
    shift_ref,
    pair_all,
    cot_all,
    left_s,
    right_s,
    tri_s,
    grad_s,
    dleft_s,
    dright_s,
    rows_s,
    send_half,
    recv_half,
    send_sum,
    recv_sum,
    small_all,
    fetch_done,
    gather_send,
    gather_recv,
    half_send,
    half_recv,
    sum_send,
    sum_recv,
    share_send,
    share_recv,
    small_send,
    small_recv,
):
    dap, dp = peers
    mesh_ids = pl.DeviceIdType.MESH
    held, channels = pair_hbm.shape
    me = lax.axis_index("dap")
    at = lax.axis_index("dp")
    core = lax.rem(at, 2)
    core_peer = at + 1 - 2 * core
    far_peer = lax.rem(at + 2, dp)

    own = pl.ds(pl.multiple_of(me * held, held), held)
    fetches = []
    for source, target in (
        (pair_hbm, pair_all.at[own]),
        (cot_hbm, cot_all.at[own]),
        (gain_hbm, gain_ref),
        (shift_hbm, shift_ref),
        (proj_hbm, proj_ref),
        (bias_hbm, bias_ref),
        (gate_hbm, gate_ref),
        (chan_hbm, chan_ref),
        (outw_hbm, outw_ref),
    ):
        copy = pltpu.make_async_copy(source, target, fetch_done.at[len(fetches)])
        copy.start()
        fetches.append(copy)

    barrier = pltpu.get_barrier_semaphore()
    for k in range(1, dap):
        pl.semaphore_signal(
            barrier, inc=1, device_id={"dap": lax.rem(me + k, dap)}, device_id_type=mesh_ids
        )
    for k in range(1, dp):
        pl.semaphore_signal(
            barrier, inc=1, device_id={"dp": lax.rem(at + k, dp)}, device_id_type=mesh_ids
        )
    pl.semaphore_wait(barrier, dap + dp - 2)

    gathers = []
    for slot, whole in enumerate((pair_all, cot_all)):
        fetches[slot].wait()
        copies = []
        for k in range(1, dap):
            copy = pltpu.make_async_remote_copy(
                src_ref=whole.at[own],
                dst_ref=whole.at[own],
                send_sem=gather_send.at[slot, k - 1],
                recv_sem=gather_recv.at[slot, k - 1],
                device_id={"dap": lax.rem(me + k, dap)},
                device_id_type=mesh_ids,
            )
            copy.start()
            copies.append(copy)
        gathers.append(copies)

    factor = 1.0 / width

    def forward(source, layer):
        normed, standard_in, inverse_in = norm_lanes(
            source, gain_ref[layer, 0:1, :], shift_ref[layer, 0:1, :]
        )
        inputs = normed.astype(jnp.bfloat16)
        pre_act = matmul_rows(inputs, proj_ref[layer]) + bias_ref[layer : layer + 1, :]
        left_value = pre_act[:, :channels]
        left_sig = jax.nn.sigmoid(pre_act[:, channels : 2 * channels])
        right_value = pre_act[:, 2 * channels : 3 * channels]
        right_sig = jax.nn.sigmoid(pre_act[:, 3 * channels :])
        left_s[layer] = rounded(left_sig * left_value)
        right_s[layer] = rounded(right_sig * right_value)
        gate = jax.nn.sigmoid(matmul_rows(inputs, gate_ref[layer]) + chan_ref[layer, 0:1, :])
        left, right = left_s.at[layer], right_s.at[layer]
        if layer == 0:
            products(width, left, False, right, True, tri_s)
        else:
            products(width, left, True, right, False, tri_s)
        normed_tri, standard_out, inverse_out = norm_lanes(
            rounded(tri_s[...]), gain_ref[layer, 1:2, :], shift_ref[layer, 1:2, :]
        )
        tri_inputs = normed_tri.astype(jnp.bfloat16)
        linear = matmul_rows(tri_inputs, outw_ref[layer]) + chan_ref[layer, 1:2, :]
        saved = (
            inputs,
            standard_in,
            inverse_in,
            left_value,
            left_sig,
            right_value,
            right_sig,
            gate,
            linear,
            tri_inputs,
            standard_out,
            inverse_out,
        )
        return saved

    def put_small(layer, row, values):
        rows_s[layer, row : row + 1, :] = values * factor

    def backward_near(upstream, saved, layer):
        inputs, _, _, _, _, _, _, gate, linear, tri_inputs, standard_out, inverse_out = saved
        grad_linear = (upstream * gate).astype(jnp.bfloat16)
        grad_logit = (upstream * linear * gate * (1.0 - gate)).astype(jnp.bfloat16)
        grad_normed = jnp.dot(grad_linear, outw_ref[layer], preferred_element_type=jnp.float32)
        grad_s[...] = rounded(
            norm_lanes_back(grad_normed, gain_ref[layer, 1:2, :], standard_out, inverse_out)
        )
        big_ref[layer, 4 * channels : 5 * channels, :] = matmul_cols(grad_logit, inputs) * factor
        big_ref[layer, 5 * channels :, :] = matmul_cols(grad_linear, tri_inputs) * factor
        put_small(layer, 4, column_sum(grad_logit.astype(jnp.float32)))
        put_small(layer, 5, column_sum(grad_linear.astype(jnp.float32)))
        put_small(layer, 7, column_sum(grad_normed * standard_out))
        put_small(layer, 9, column_sum(grad_normed))
        return grad_logit

    def backward_far(upstream, saved, grad_logit, layer):
        inputs, standard_in, inverse_in, left_value, left_sig, right_value, right_sig = saved[:7]
        left, right = left_s.at[layer], right_s.at[layer]
        if layer == 0:
            products(width, grad_s, False, right, False, dleft_s)
            products(width, grad_s, True, left, False, dright_s)
        else:
            products(width, right, False, grad_s, True, dleft_s)
            products(width, left, False, grad_s, False, dright_s)
        left_back = rounded(dleft_s[...])
        right_back = rounded(dright_s[...])
        blocks = (
            left_back * left_sig,
            left_back * left_value * left_sig * (1.0 - left_sig),
            right_back * right_sig,
            right_back * right_value * right_sig * (1.0 - right_sig),
        )
        grad_inputs = jnp.dot(grad_logit, gate_ref[layer], preferred_element_type=jnp.float32)
        for index, block in enumerate(blocks):
            part = block.astype(jnp.bfloat16)
            lines = slice(index * channels, (index + 1) * channels)
            big_ref[layer, lines, :] = matmul_cols(part, inputs) * factor
            put_small(layer, index, column_sum(part.astype(jnp.float32)))
            grad_inputs = grad_inputs + jnp.dot(
                part, proj_ref[layer, lines, :], preferred_element_type=jnp.float32
            )
            if index == 0 and layer == 0:
                exchange_sum(1)
            if index % 2 == 1 and layer == 0:
                exchange_half(2 + index // 2)
        put_small(layer, 6, column_sum(grad_inputs * standard_in))
        put_small(layer, 8, column_sum(grad_inputs))
        return upstream + norm_lanes_back(
            grad_inputs, gain_ref[layer, 0:1, :], standard_in, inverse_in
        )

    pieces = (
        (1, 0, 6 * channels),
        (0, 4 * channels, 2 * channels),
        (0, 0, 2 * channels),
        (0, 2 * channels, 2 * channels),
    )
    flights = {}

    def spans(index):
        layer, first, count = pieces[index]
        half = count // 2
        mine = pl.ds(pl.multiple_of(first + core * half, half), half)
        other = pl.ds(pl.multiple_of(first + (1 - core) * half, half), half)
        slot = pl.ds(sum(piece[2] // 2 for piece in pieces[:index]), half)
        return (big_ref.at[layer], mine, other, slot)

    def exchange_half(index):
        whole, mine, other, slot = spans(index)
        send_half[slot, :] = whole[other, :].astype(jnp.bfloat16)
        copy = pltpu.make_async_remote_copy(
            src_ref=send_half.at[slot],
            dst_ref=recv_half.at[slot],
            send_sem=half_send.at[index],
            recv_sem=half_recv.at[index],
            device_id={"dp": core_peer},
            device_id_type=mesh_ids,
        )
        copy.start()
        flights[index] = [copy]

    def exchange_sum(index):
        whole, mine, other, slot = spans(index)
        flights[index][0].wait_recv()
        added = whole[mine, :] + recv_half[slot, :].astype(jnp.float32)
        send_sum[slot, :] = added.astype(jnp.bfloat16)
        copy = pltpu.make_async_remote_copy(
            src_ref=send_sum.at[slot],
            dst_ref=recv_sum.at[slot],
            send_sem=sum_send.at[index],
            recv_sem=sum_recv.at[index],
            device_id={"dp": far_peer},
            device_id_type=mesh_ids,
        )
        copy.start()
        flights[index].append(copy)

    def share(index):
        whole, mine, other, slot = spans(index)
        flights[index][1].wait_recv()
        whole[mine, :] = send_sum[slot, :].astype(jnp.float32) + recv_sum[slot, :].astype(
            jnp.float32
        )
        copy = pltpu.make_async_remote_copy(
            src_ref=whole.at[mine],
            dst_ref=whole.at[mine],
            send_sem=share_send.at[index],
            recv_sem=share_recv.at[index],
            device_id={"dp": core_peer},
            device_id_type=mesh_ids,
        )
        copy.start()
        flights[index].append(copy)

    for copy in fetches[2:]:
        copy.wait()
    for copy in gathers[0]:
        copy.wait_recv()
    start_pair = pair_all[...].astype(jnp.float32)
    saved_first = forward(start_pair, 0)
    middle = rounded(start_pair + saved_first[7] * saved_first[8])
    saved_second = forward(middle, 1)
    for copy in gathers[1]:
        copy.wait_recv()
    upstream = cot_all[...].astype(jnp.float32)
    grad_logit = backward_near(upstream, saved_second, 1)
    grad_middle = backward_far(upstream, saved_second, grad_logit, 1)
    exchange_half(0)
    grad_logit = backward_near(grad_middle, saved_first, 0)
    exchange_half(1)
    exchange_sum(0)
    grad_start = backward_far(grad_middle, saved_first, grad_logit, 0)
    small_all[at] = rows_s[...]
    small_copies = []
    for k in range(1, dp):
        copy = pltpu.make_async_remote_copy(
            src_ref=rows_s,
            dst_ref=small_all.at[at],
            send_sem=small_send.at[k - 1],
            recv_sem=small_recv.at[k - 1],
            device_id={"dp": lax.rem(at + k, dp)},
            device_id_type=mesh_ids,
        )
        copy.start()
        small_copies.append(copy)
    exchange_sum(2)
    exchange_sum(3)
    dleft_s[...] = grad_start
    dpair_ref[...] = dleft_s[own, :].astype(jnp.bfloat16)
    share(0)
    share(1)
    for copy in small_copies:
        copy.wait_recv()
    total = small_all[0]
    for index in range(1, dp):
        total = total + small_all[index]
    for index in range(4):
        dbias_ref[:, index * channels : (index + 1) * channels] = total[:, index]
    dchan_ref[...] = total[:, 4:6]
    dgain_ref[...] = total[:, 6:8]
    dshift_ref[...] = total[:, 8:10]
    share(2)
    share(3)
    for index in range(4):
        flights[index][2].wait_recv()
    for index in range(4):
        for copy in flights[index]:
            copy.wait_send()
    for copy in gathers[0] + gathers[1] + small_copies:
        copy.wait_send()


def deliver_kernel(
    dpair_ref,
    big_ref,
    dbias_ref,
    dchan_ref,
    dgain_ref,
    dshift_ref,
    dpair_out,
    proj_out,
    bias_out,
    gate_out,
    outw_out,
    chan_out,
    gain_out,
    shift_out,
    done,
):
    channels = big_ref.shape[2]
    copies = []
    for source, target in (
        (big_ref.at[:, : 4 * channels], proj_out),
        (big_ref.at[:, 4 * channels : 5 * channels], gate_out),
        (big_ref.at[:, 5 * channels :], outw_out),
        (dpair_ref, dpair_out),
        (dbias_ref, bias_out),
        (dchan_ref, chan_out),
        (dgain_ref, gain_out),
        (dshift_ref, shift_out),
    ):
        copy = pltpu.make_async_copy(source, target, done.at[len(copies)])
        copy.start()
        copies.append(copy)
    for copy in copies:
        copy.wait()


def fused_body(
    peers,
    pair,
    cotangent,
    proj_weight,
    proj_bias,
    gate_weight,
    out_weight,
    chan_bias,
    norm_gain,
    norm_shift,
):
    dap, dp = peers
    _, channels, rows, width = pair.shape
    held = rows * width
    entries = width * width
    float_rows = pltpu.VMEM((entries, channels), jnp.float32)
    layer_rows = pltpu.VMEM((2, entries, channels), jnp.float32)
    half_rows = pltpu.VMEM((6 * channels, channels), jnp.bfloat16)
    vmem = pl.BlockSpec(memory_space=pltpu.VMEM)
    hbm = pl.BlockSpec(memory_space=pltpu.HBM)
    summed = pl.pallas_call(
        functools.partial(fused_kernel, peers, width),
        out_shape=(
            pltpu.VMEM((held, channels), jnp.bfloat16),
            pltpu.VMEM((2, 6 * channels, channels), jnp.float32),
            pltpu.VMEM((2, 4 * channels), jnp.float32),
            pltpu.VMEM((2, 2, channels), jnp.float32),
            pltpu.VMEM((2, 2, channels), jnp.float32),
            pltpu.VMEM((2, 2, channels), jnp.float32),
        ),
        in_specs=[hbm] * 9,
        out_specs=(vmem,) * 6,
        scratch_shapes=[
            pltpu.VMEM(proj_weight.shape, jnp.bfloat16),
            pltpu.VMEM(gate_weight.shape, jnp.bfloat16),
            pltpu.VMEM(out_weight.shape, jnp.bfloat16),
            pltpu.VMEM(proj_bias.shape, jnp.float32),
            pltpu.VMEM(chan_bias.shape, jnp.float32),
            pltpu.VMEM(norm_gain.shape, jnp.float32),
            pltpu.VMEM(norm_shift.shape, jnp.float32),
            pltpu.VMEM((entries, channels), jnp.bfloat16),
            pltpu.VMEM((entries, channels), jnp.bfloat16),
            layer_rows,
            layer_rows,
            float_rows,
            float_rows,
            float_rows,
            float_rows,
            pltpu.VMEM((2, 10, channels), jnp.float32),
            half_rows,
            half_rows,
            half_rows,
            half_rows,
            pltpu.VMEM((dp, 2, 10, channels), jnp.float32),
            pltpu.SemaphoreType.DMA((9,)),
            pltpu.SemaphoreType.DMA((2, dap - 1)),
            pltpu.SemaphoreType.DMA((2, dap - 1)),
            pltpu.SemaphoreType.DMA((4,)),
            pltpu.SemaphoreType.DMA((4,)),
            pltpu.SemaphoreType.DMA((4,)),
            pltpu.SemaphoreType.DMA((4,)),
            pltpu.SemaphoreType.DMA((4,)),
            pltpu.SemaphoreType.DMA((4,)),
            pltpu.SemaphoreType.DMA((dp - 1,)),
            pltpu.SemaphoreType.DMA((dp - 1,)),
        ],
        compiler_params=pltpu.CompilerParams(
            collective_id=0, has_side_effects=True, vmem_limit_bytes=60 * 1024 * 1024
        ),
        name="triangle_updates",
    )(
        pair[0].reshape(channels, held).T,
        cotangent[0].reshape(channels, held).T,
        proj_weight,
        gate_weight,
        out_weight,
        proj_bias,
        chan_bias,
        norm_gain,
        norm_shift,
    )
    outputs = pl.pallas_call(
        deliver_kernel,
        out_shape=(
            jax.ShapeDtypeStruct((held, channels), jnp.bfloat16),
            jax.ShapeDtypeStruct((2, 4 * channels, channels), jnp.float32),
            jax.ShapeDtypeStruct((2, 4 * channels), jnp.float32),
            jax.ShapeDtypeStruct((2, channels, channels), jnp.float32),
            jax.ShapeDtypeStruct((2, channels, channels), jnp.float32),
            jax.ShapeDtypeStruct((2, 2, channels), jnp.float32),
            jax.ShapeDtypeStruct((2, 2, channels), jnp.float32),
            jax.ShapeDtypeStruct((2, 2, channels), jnp.float32),
        ),
        in_specs=[vmem] * 6,
        out_specs=(hbm,) * 8,
        scratch_shapes=[pltpu.SemaphoreType.DMA((8,))],
        compiler_params=pltpu.CompilerParams(vmem_limit_bytes=4 * 1024 * 1024),
        name="deliver",
    )(*summed)
    return (outputs[0].T.reshape(1, channels, rows, width),) + tuple(outputs[1:])


def any_body(peers, pair, *others):
    _, channels, rows, width = pair.shape
    small = channels == 128 and width == 16 and rows % 4 == 0
    if small and peers[1] == 4 and peers[0] > 1:
        return fused_body(peers, pair, *others)
    return large_body(pair, *others)


def solution(mesh):
    in_specs = (
        P(("groups", "dp"), None, "dap", None),
        P(("groups", "dp"), None, "dap", None),
        P(),
        P(),
        P(),
        P(),
        P(),
        P(),
        P(),
    )
    out_specs = (
        P(("groups", "dp"), None, "dap", None),
        P("groups", None, None),
        P("groups", None),
        P("groups", None, None),
        P("groups", None, None),
        P("groups", None, None),
        P("groups", None, None),
        P("groups", None, None),
    )
    peers = (mesh.shape["dap"], mesh.shape["dp"])
    body = functools.partial(any_body, peers)
    return jax.shard_map(body, mesh=mesh, in_specs=in_specs, out_specs=out_specs, check_vma=False)
```
